32 devices in a mesh: groups: 2 (over x), fsdp: 16 (over z, y, core).
Axes of the slice: x: 2, y: 2, z: 4, core: 2. Of those that a mesh axis runs over, the one named last changes fastest.
Arguments:
- hidden: bfloat16 [4096, 8192], P(('groups', 'fsdp')), parts along dimension 0, may hold values from -6 to 6
- output_gradient: bfloat16 [4096, 512], P(('groups', 'fsdp')), parts along dimension 0, may hold values from -6 to 6
- frozen_value_weight: bfloat16 [8192, 512], P('fsdp'), may hold values from -0.0625 to 0.0625
- adapter_down_maps: bfloat16 [16, 8192, 32], P('fsdp'), may hold values from -0.0625 to 0.0625
- adapter_up_maps: bfloat16 [16, 32, 512], P('fsdp'), may hold values from -1 to 1
- owner: int32 [16], replicated, may hold values from 0 to 15, each once
- token_block_tenant: int32 [32, 1], P(('groups', 'fsdp')), parts along dimension 0, may hold values from 0 to 15
Outputs:
- values: bfloat16 [4096, 512], P(('groups', 'fsdp')), parts along dimension 0
- grad_hidden: bfloat16 [4096, 8192], P(('groups', 'fsdp')), parts along dimension 0
- grad_down: float32 [32, 8192, 32], P(('groups', 'fsdp')), parts along dimension 0
- up_map_gradient: float32 [32, 32, 512], P(('groups', 'fsdp')), parts along dimension 0
The draws below stay inside these ranges and needn't reach their ends.
There are 2 independent parts, one for each index of `groups`. The reference program is written for one: setup_inputs(seed, part) draws one part's arguments, and reference() takes and returns one part's arrays. A program takes and returns all parts, laid end to end along the dimension named above; an argument that names none is the same for every part. Nothing has to cross between parts.
Inputs may be any that keep to these rules, and one draw needn't show every extreme that they name: `owner`: each tenant has exactly one slot, each slot one tenant.
All inputs are finite; a program needn't handle non-finite values.
Results may differ from the reference program's by a relative error of at most 0.0055.
Values may be sent and summed in bfloat16 or wider, within the bound.
A program may use at most 128 MiB of HBM per device.

```python
import math
import jax
import jax.numpy as jnp
import numpy as np

MODEL_DIM = 8192
VALUE_OUTPUTS = 512
ADAPTER_RANK = 32
BLK = 128
TOKENS = 2048
TENANT_SLOTS = 16


def place_ends(values, key, smallest, top_value):
    longest = values.shape.index(max(values.shape))
    spots = []
    for shift in (0, 1):
        where = [jax.random.randint(jax.random.fold_in(key, axis), (), 0, length) for axis, length in enumerate(values.shape)]
        where[longest] = (where[longest] + shift) % values.shape[longest]
        spots.append(tuple(where))
    return values.at[spots[0]].set(smallest).at[spots[1]].set(top_value)


def level_of(key, extent, split, least, top_value):
    loudness = 1.0
    for position, shards_of in split:
        draws = jax.random.uniform(jax.random.fold_in(jax.random.fold_in(key, 6), position), (shards_of,), jnp.float32, least / len(split), top_value / len(split))
        loudness = loudness * jnp.repeat(jnp.exp(draws), extent[position] // shards_of).reshape((-1,) + (1,) * (len(extent) - 1 - position))
    return loudness


def rank_table(number_of, slope):
    portions = [(1 << 20) // math.isqrt(standing ** slope) + 1 for standing in range(1, number_of + 1)]
    spread = 1 + sum(portions) // (1 << 30)
    return np.cumsum(np.array([max(1, weight // spread) for weight in portions]))


def ranked_ids(own_key, dims, amount, lean):
    grid = rank_table(amount, lean)
    pick = jax.random.randint(jax.random.fold_in(own_key, 1), dims, 0, int(grid[amount - 1]))
    grade = jnp.searchsorted(jnp.asarray(grid, jnp.int32), pick, side="right")
    return jax.random.permutation(jax.random.fold_in(own_key, 2), amount)[grade].astype(jnp.int32)


def noise(own_key, shape, scale, limit, pieces=(), held_as=jnp.bfloat16):
    gain = level_of(own_key, shape, pieces, -0.22, 0.18) if pieces else 1.0
    drawn = jax.random.normal(own_key, shape, jnp.float32) * scale * gain
    return jnp.minimum(jnp.maximum(drawn, -limit), limit).astype(held_as)


def setup_inputs(seed: int = 0, part: int = 0) -> dict:
    arg_keys = jax.random.split(jax.random.key(seed), 8)
    part_keys = jax.random.split(jax.random.fold_in(arg_keys[7], part), 8)
    hidden = noise(part_keys[0], (TOKENS, MODEL_DIM), 1.0, 6.0, ((0, 16),))
    output_gradient = noise(part_keys[1], (TOKENS, VALUE_OUTPUTS), 1.0, 6.0, ((0, 16),))
    frozen_value_weight = noise(arg_keys[2], (MODEL_DIM, VALUE_OUTPUTS), MODEL_DIM ** -0.5, 0.0625, ((0, 16),))
    adapter_down_maps = noise(arg_keys[3], (TENANT_SLOTS, MODEL_DIM, ADAPTER_RANK), MODEL_DIM ** -0.5, 0.0625, ((0, 16),))
    adapter_up_maps = noise(arg_keys[4], (TENANT_SLOTS, ADAPTER_RANK, VALUE_OUTPUTS), ADAPTER_RANK ** -0.5, 1.0, ((0, 16),))
    owner = jax.random.permutation(arg_keys[5], TENANT_SLOTS).astype(jnp.int32)
    token_block_tenant = place_ends(ranked_ids(part_keys[6], (TOKENS // BLK, 1), TENANT_SLOTS, 2), jax.random.fold_in(part_keys[6], 3), 0, TENANT_SLOTS - 1).astype(jnp.int32)
    return {"hidden": hidden, "output_gradient": output_gradient, "frozen_value_weight": frozen_value_weight, "adapter_down_maps": adapter_down_maps, "adapter_up_maps": adapter_up_maps, "owner": owner, "token_block_tenant": token_block_tenant}


adapter_scale = 2.0


def reference(hidden, output_gradient, frozen_value_weight, adapter_down_maps, adapter_up_maps, owner, token_block_tenant):
    block_count = hidden.shape[0] // BLK
    tenant_slot_list = owner[token_block_tenant[:, 0]].astype(jnp.int32)
    token_block_list = hidden.reshape(block_count, BLK, MODEL_DIM).astype(jnp.float32)
    gradient_block_list = output_gradient.reshape(block_count, BLK, VALUE_OUTPUTS).astype(jnp.float32)
    down_map_blocks = adapter_down_maps[tenant_slot_list].astype(jnp.float32)
    up_map_blocks = adapter_up_maps[tenant_slot_list].astype(jnp.float32)
    reduced_projection = jnp.einsum("vxh,vht->vxt", token_block_list, down_map_blocks).astype(jnp.bfloat16)
    frozen_output = jnp.dot(hidden, frozen_value_weight, preferred_element_type=jnp.float32)
    adapter_output = jnp.einsum("bkr,brv->bkv", reduced_projection.astype(jnp.float32), up_map_blocks).reshape(-1, VALUE_OUTPUTS)
    values = (frozen_output + adapter_scale * adapter_output).astype(jnp.bfloat16)
    backward_low_rank = (adapter_scale * jnp.einsum("jui,jti->jut", gradient_block_list, up_map_blocks)).astype(jnp.bfloat16)
    adapter_gradient = jnp.einsum("jsn,jwn->jsw", backward_low_rank.astype(jnp.float32), down_map_blocks).astype(jnp.bfloat16)
    base_grad = jnp.einsum("kv,dv->kd", output_gradient.astype(jnp.float32), frozen_value_weight.astype(jnp.float32))
    grad_hidden = (base_grad + adapter_gradient.reshape(-1, MODEL_DIM).astype(jnp.float32)).astype(jnp.bfloat16)
    block_down_map = jnp.einsum("fmy,fmo->fyo", token_block_list, backward_low_rank.astype(jnp.float32))
    grad_down = jax.ops.segment_sum(block_down_map, tenant_slot_list, num_segments=TENANT_SLOTS)
    block_up_map = jnp.einsum("bkr,bkv->brv", reduced_projection.astype(jnp.float32), gradient_block_list)
    up_map_gradient = adapter_scale * jax.ops.segment_sum(block_up_map, tenant_slot_list, num_segments=TENANT_SLOTS)
    return values, grad_hidden, grad_down, up_map_gradient
```

```python
import functools

import jax
import jax.numpy as jnp
from jax import lax
from jax.experimental import pallas as pl
from jax.experimental.pallas import tpu as pltpu
from jax.sharding import PartitionSpec as P

MESH = pl.DeviceIdType.MESH
adapter_scale = 2.0
F32 = jnp.float32
BF16 = jnp.bfloat16


def dot(a, b, over):
    return lax.dot_general(a, b, ((over[:1], over[1:]), ((), ())), preferred_element_type=F32)


class Ring:
    def __init__(self, place, pool, buf, axis, shared):
        self.place, self.pool, self.buf, self.axis = place, pool, buf, axis
        length = buf.shape[axis]
        self.shared = shared
        self.length = length // 2 if shared else length
        self.start_at = place["side"] * self.length if shared else 0
        self.other_at = (1 - place["side"]) * self.length if shared else 0
        self.right, self.left, self.twin, self.near = {}, {}, {}, {}
        self.near_twin = {}

    def view(self, index, start, length):
        if self.axis == 1:
            return self.buf.at[index, pl.ds(pl.multiple_of(start, 16), length), :]
        return self.buf.at[index, :, pl.ds(pl.multiple_of(start, 128), length)]

    def send(self, index, start, length, to):
        ref = self.view(index, start, length)
        return self.pool(ref, to)

    def chip(self, offset):
        place = self.place
        return place["chip_at"](lax.rem(place["spot"] + offset + place["chips"], place["chips"]))

    def mine(self, offset):
        return self.chip(offset) * 2 + self.place["core"]

    def begin(self):
        place = self.place
        self.near[0] = [self.send(place["me"], 0, self.buf.shape[self.axis], place["near"])]
        self.right[1] = self.send(place["me"], self.start_at, self.length, place["right"])
        self.left[1] = self.send(place["me"], self.start_at, self.length, place["left"])

    def step(self, k):
        place, half = self.place, self.length // 2
        last = place["chips"] // 2
        from_left, from_right = self.mine(-k), self.mine(k)
        self.right[k].wait_recv()
        if k + 1 <= last:
            size = self.length if k + 1 < last else half
            self.right[k + 1] = self.send(from_left, self.start_at, size, place["right"])
        self.left[k].wait_recv()
        if k + 1 <= last:
            size = self.length if k + 1 < last else half
            self.left[k + 1] = self.send(
                from_right, self.start_at + self.length - size, size, place["left"]
            )
        got = [from_left, from_right] if k < last else [from_left]
        if self.shared:
            self.twin[k] = [self.send(i, self.start_at, self.length, place["twin"]) for i in got]
        self.near[k] = [self.send(i, self.start_at, self.length, place["near"]) for i in got]

    def cross(self, k):
        place, last = self.place, self.place["chips"] // 2
        got = [self.mine(-k), self.mine(k)] if k < last else [self.mine(-k)]
        self.near_twin[k] = []
        for i, copy in zip(got, self.twin[k]):
            copy.wait_recv()
            self.near_twin[k].append(self.send(i, self.other_at, self.length, place["near"]))

    def settle(self, k):
        for copy in self.near[k]:
            copy.wait_recv()
        for copy in self.near_twin.get(k, []):
            copy.wait_recv()


def copies_of(chips, shared):
    last = chips // 2
    got = 2 * last - 1
    return 1 + 2 * last + got * (3 if shared else 1)


def kernel(
    n, ring_of, staged,
    slot_ref, hidden, gradient, weight, down, up,
    values, grad_hidden, grad_down, grad_up, *rest,
):
    if staged:
        parts, w_all, d_all, u_all, t_all, back, stage, send_sems, recv_sems, local_sems = rest
    else:
        parts, w_all, d_all, u_all, t_all, back, send_sems, recv_sems, local_sems = rest
    me = lax.axis_index("fsdp")
    group = lax.axis_index("groups")
    chips, last = n // 2, n // 4
    core, chip = lax.rem(me, 2), me // 2
    chip_at, spot_of = ring_of
    spot = spot_of(chip)
    side = lax.rem(group, 2)

    def device(at):
        return (group, chip_at(lax.rem(spot + at + chips, chips)) * 2 + core)

    place = {
        "me": me, "core": core, "spot": spot, "side": side, "chips": chips, "chip_at": chip_at,
        "right": device(1), "left": device(-1),
        "near": (group, chip * 2 + 1 - core), "twin": (group + 1 - 2 * side, me),
    }
    local = [
        pltpu.make_async_copy(src, dst.at[me], local_sems.at[i])
        for i, (src, dst) in enumerate(((up, u_all), (down, d_all), (weight, w_all)))
    ]
    for copy in local:
        copy.start()

    barrier = pltpu.get_barrier_semaphore()
    for to in ("right", "left", "near", "twin"):
        pl.semaphore_signal(barrier, inc=1, device_id=place[to], device_id_type=MESH)
    pl.semaphore_wait(barrier, 4)

    sent = []

    def pool(ref, to):
        i = len(sent)
        copy = pltpu.make_async_remote_copy(
            src_ref=ref, dst_ref=ref, send_sem=send_sems.at[i], recv_sem=recv_sems.at[i],
            device_id=to, device_id_type=MESH,
        )
        copy.start()
        sent.append(copy)
        return copy

    ups = Ring(place, pool, u_all, 2, False)
    downs = Ring(place, pool, d_all, 2, True)
    weights = Ring(place, pool, w_all, 1, True)
    terms = Ring(place, pool, parts, 2, False)
    up_terms = Ring(place, pool, t_all, 2, False)

    local[0].wait()
    ups.begin()
    local[1].wait()
    downs.begin()
    for k in range(1, last + 1):
        ups.step(k)
        if k == 1:
            local[2].wait()
            weights.begin()
    for k in range(last + 1):
        ups.settle(k)

    rank, width = down.shape
    tile = 1024
    slot = slot_ref[0]
    up_slot = u_all[slot][:rank, :]
    back_low = (adapter_scale * dot(gradient[...], up_slot, (1, 1))).astype(BF16)
    back[...] = back_low
    back_turned = back_low.astype(F32).T.astype(BF16)
    mine = stage if staged else parts.at[me]

    @pl.loop(0, width // tile)
    def _(t):
        at = pl.ds(pl.multiple_of(t * tile, tile), tile)
        term = dot(back_turned, hidden[:, at], (1, 0))
        mine[:, at] = term.astype(BF16)
        grad_down[:, at] = jnp.zeros((rank, tile), F32)

    if staged:
        out = pltpu.make_async_copy(stage, parts.at[me], local_sems.at[3])
        out.start()
        out.wait()
    terms.begin()

    def chunk(offset, which):
        return chip_at(lax.rem(spot + offset + chips, chips)) * 2 + which

    def share(j):
        return (u_all[j][rank:rank + 1, 0:1].astype(F32) == me.astype(F32)).astype(F32)

    def add_terms(i, first):
        j = chunk(i // 2 + first, lax.rem(i, 2))
        weight_of = share(j)
        if staged:
            get = pltpu.make_async_copy(parts.at[j], stage, local_sems.at[3])
            get.start()
            get.wait()

        @pl.loop(0, width // tile)
        def _(t):
            at = pl.ds(pl.multiple_of(t * tile, tile), tile)
            term = stage[:, at] if staged else parts[j, :, at]
            grad_down[:, at] += weight_of * term.astype(F32)

    rows = w_all.shape[1]

    def apply_weight(i, total, first):
        j = chunk(i // 2 + first, lax.rem(i, 2))
        at = pl.ds(pl.multiple_of(j * rows, 128), rows)
        block = w_all[j]
        base = dot(gradient[...], block, (1, 1))
        grad_hidden[:, at] = (base + grad_hidden[:, at].astype(F32)).astype(BF16)
        return total + dot(hidden[:, at], block, (1, 0))

    for k in range(1, last + 1):
        downs.step(k)
        if k > 1:
            weights.step(k - 1)
            terms.step(k - 1)
        downs.cross(k)
        if k > 1:
            weights.cross(k - 1)
    for k in range(last + 1):
        downs.settle(k)

    def low_part(t, total):
        at = pl.ds(pl.multiple_of(t * tile, tile), tile)
        piece = d_all[slot, :, at]
        grad_hidden[:, at] = dot(back[...], piece, (1, 0)).astype(BF16)
        return total + dot(hidden[:, at], piece, (1, 1))

    low = lax.fori_loop(0, width // tile, low_part, jnp.zeros((hidden.shape[0], rank), F32))
    low_turned = low.astype(BF16).astype(F32).T.astype(BF16)
    t_all[me] = (adapter_scale * dot(low_turned, gradient[...], (1, 0))).astype(BF16)
    up_terms.begin()
    total = adapter_scale * dot(low.astype(BF16), u_all[slot][:rank, :], (1, 0))

    for k in range(1, last + 1):
        up_terms.step(k)
        if k == 1:
            weights.step(last)
            terms.step(last)
            weights.cross(last)
    for k in range(last):
        weights.settle(k)
        terms.settle(k)
    before = 2 * (2 * last - 1)
    total = lax.fori_loop(0, before, functools.partial(apply_weight, first=1 - last), total)

    @pl.loop(0, before)
    def _(i):
        add_terms(i, 1 - last)

    weights.settle(last)
    total = lax.fori_loop(0, 2, functools.partial(apply_weight, first=last), total)
    values[...] = total.astype(BF16)
    terms.settle(last)

    @pl.loop(0, 2)
    def _(i):
        add_terms(i, last)

    for k in range(last + 1):
        up_terms.settle(k)
    grad_up[...] = lax.fori_loop(
        0, n, lambda j, held: held + share(j) * t_all[j].astype(F32),
        jnp.zeros(grad_up.shape, F32),
    )
    for copy in sent:
        copy.wait_send()


def ring_order(chips):
    if chips == 8:
        return (
            lambda p: jnp.where(p < 4, 2 * p, 2 * (7 - p) + 1),
            lambda c: jnp.where(lax.rem(c, 2) == 0, c // 2, 7 - c // 2),
        )
    return (lambda p: p, lambda c: c)


def per_device(
    hidden,
    output_gradient,
    frozen_value_weight,
    adapter_down_maps,
    adapter_up_maps,
    owner,
    token_block_tenant,
):
    n = lax.axis_size("fsdp")
    chips = n // 2
    rows, width = hidden.shape
    outputs = output_gradient.shape[1]
    rank = adapter_down_maps.shape[2]
    tenants = owner.shape[0]
    staged = n > 16
    slot = jnp.sum(
        jnp.where(token_block_tenant[0, 0] == jnp.arange(tenants, dtype=jnp.int32), owner, 0)
    )
    up = jnp.concatenate(
        [adapter_up_maps[0], jnp.broadcast_to(slot.astype(BF16), (16, outputs))], axis=0
    )
    down = adapter_down_maps[0].T
    count = 2 * copies_of(chips, True) + 3 * copies_of(chips, False)
    vmem = pl.BlockSpec(memory_space=pltpu.VMEM)
    hbm = pl.BlockSpec(memory_space=pl.ANY)
    out_shape = [
        jax.ShapeDtypeStruct((rows, outputs), BF16),
        jax.ShapeDtypeStruct((rows, width), BF16),
        jax.ShapeDtypeStruct((rank, width), F32),
        jax.ShapeDtypeStruct((rank, outputs), F32),
    ]
    out_specs = [vmem] * 4
    scratch = []
    if staged:
        out_shape.append(jax.ShapeDtypeStruct((n, rank, width), BF16))
        out_specs.append(hbm)
    else:
        scratch.append(pltpu.VMEM((n, rank, width), BF16))
    scratch += [
        pltpu.VMEM((n,) + frozen_value_weight.shape, BF16),
        pltpu.VMEM((n, rank, width), BF16),
        pltpu.VMEM((n,) + up.shape, BF16),
        pltpu.VMEM((n, rank, outputs), BF16),
        pltpu.VMEM((rows, rank), BF16),
    ]
    if staged:
        scratch.append(pltpu.VMEM((rank, width), BF16))
    scratch += [
        pltpu.SemaphoreType.DMA((count,)),
        pltpu.SemaphoreType.DMA((count,)),
        pltpu.SemaphoreType.DMA((4,)),
    ]
    results = pl.pallas_call(
        functools.partial(kernel, n, ring_order(chips), staged),
        out_shape=out_shape,
        in_specs=[pl.BlockSpec(memory_space=pltpu.SMEM), vmem, vmem, hbm, hbm, hbm],
        out_specs=out_specs,
        scratch_shapes=scratch,
        compiler_params=pltpu.CompilerParams(
            collective_id=0, has_side_effects=True, vmem_limit_bytes=56 << 20
        ),
    )(slot.reshape(1), hidden, output_gradient, frozen_value_weight, down, up)
    values, grad_hidden, grad_down, grad_up = results[:4]
    return values, grad_hidden, grad_down.T[None], grad_up[None]


def solution(mesh):
    return jax.shard_map(
        per_device,
        mesh=mesh,
        in_specs=(
            P(("groups", "fsdp"), None),
            P(("groups", "fsdp"), None),
            P("fsdp", None),
            P("fsdp", None, None),
            P("fsdp", None, None),
            P(),
            P(("groups", "fsdp"), None),
        ),
        out_specs=(
            P(("groups", "fsdp"), None),
            P(("groups", "fsdp"), None),
            P(("groups", "fsdp"), None, None),
            P(("groups", "fsdp"), None, None),
        ),
        check_vma=False,
    )
```

```python
import functools

import jax
import jax.numpy as jnp
from jax import lax
from jax.experimental import pallas as pl
from jax.experimental.pallas import tpu as pltpu
from jax.sharding import PartitionSpec as P

MESH = pl.DeviceIdType.MESH
adapter_scale = 2.0
F32 = jnp.float32
BF16 = jnp.bfloat16


def dot(a, b, over):
    return lax.dot_general(a, b, ((over[:1], over[1:]), ((), ())), preferred_element_type=F32)


class Ring:
    def __init__(self, place, pool, buf, axis, shared):
        self.place, self.pool, self.buf, self.axis = place, pool, buf, axis
        length = buf.shape[axis]
        self.shared = shared
        self.length = length // 2 if shared else length
        self.start_at = place["side"] * self.length if shared else 0
        self.other_at = (1 - place["side"]) * self.length if shared else 0
        self.right, self.left, self.twin, self.near = {}, {}, {}, {}
        self.near_twin = {}

    def view(self, index, start, length):
        if self.axis == 1:
            return self.buf.at[index, pl.ds(pl.multiple_of(start, 16), length), :]
        return self.buf.at[index, :, pl.ds(pl.multiple_of(start, 128), length)]

    def send(self, index, start, length, to):
        ref = self.view(index, start, length)
        return self.pool(ref, to)

    def chip(self, offset):
        place = self.place
        return place["chip_at"](lax.rem(place["spot"] + offset + place["chips"], place["chips"]))

    def mine(self, offset):
        return self.chip(offset) * 2 + self.place["core"]

    def begin(self):
        place = self.place
        self.near[0] = [self.send(place["me"], 0, self.buf.shape[self.axis], place["near"])]
        self.right[1] = self.send(place["me"], self.start_at, self.length, place["right"])
        self.left[1] = self.send(place["me"], self.start_at, self.length, place["left"])

    def step(self, k, hold_twin=False):
        place, half = self.place, self.length // 2
        last = place["chips"] // 2
        from_left, from_right = self.mine(-k), self.mine(k)
        self.right[k].wait_recv()
        if k + 1 <= last:
            size = self.length if k + 1 < last else half
            self.right[k + 1] = self.send(from_left, self.start_at, size, place["right"])
        self.left[k].wait_recv()
        if k + 1 <= last:
            size = self.length if k + 1 < last else half
            self.left[k + 1] = self.send(
                from_right, self.start_at + self.length - size, size, place["left"]
            )
        got = [from_left, from_right] if k < last else [from_left]
        if self.shared and not hold_twin:
            self.to_twin(k)
        self.near[k] = [self.send(i, self.start_at, self.length, place["near"]) for i in got]

    def got(self, k):
        return [self.mine(-k), self.mine(k)] if k < self.place["chips"] // 2 else [self.mine(-k)]

    def to_twin(self, k):
        to = self.place["twin"]
        self.twin[k] = [self.send(i, self.start_at, self.length, to) for i in self.got(k)]

    def cross(self, k):
        place, got = self.place, self.got(k)
        self.near_twin[k] = []
        for i, copy in zip(got, self.twin[k]):
            copy.wait_recv()
            self.near_twin[k].append(self.send(i, self.other_at, self.length, place["near"]))

    def settle(self, k):
        for copy in self.near[k]:
            copy.wait_recv()
        for copy in self.near_twin.get(k, []):
            copy.wait_recv()


class Direct:
    def __init__(self, place, pool, buf):
        self.place, self.pool, self.buf = place, pool, buf

    def begin(self):
        place = self.place
        ref = self.buf.at[place["me"]]
        self.far = [self.pool(ref, to) for to in place["peers"]]
        self.near = [self.pool(ref, place["near"])]

    def pass_on(self):
        chips = self.place["chips"]
        for offset, copy in enumerate(self.far, 1):
            copy.wait_recv()
            spot = lax.rem(self.place["spot"] - offset + chips, chips)
            ref = self.buf.at[self.place["chip_at"](spot) * 2 + self.place["core"]]
            self.near.append(self.pool(ref, self.place["near"]))

    def settle(self):
        for copy in self.near:
            copy.wait_recv()


def copies_of(chips, shared):
    last = chips // 2
    got = 2 * last - 1
    return 1 + 2 * last + got * (3 if shared else 1)


def kernel(
    n, ring_of, staged,
    slot_ref, hidden, gradient, weight, down, up,
    values, grad_hidden, grad_down, grad_up, *rest,
):
    if staged:
        parts, w_all, d_all, u_all, t_all, back, stage, send_sems, recv_sems, local_sems = rest
    else:
        parts, w_all, d_all, u_all, t_all, back, send_sems, recv_sems, local_sems = rest
    me = lax.axis_index("fsdp")
    group = lax.axis_index("groups")
    chips, last = n // 2, n // 4
    core, chip = lax.rem(me, 2), me // 2
    chip_at, spot_of = ring_of
    spot = spot_of(chip)
    side = lax.rem(group, 2)

    def device(at):
        return (group, chip_at(lax.rem(spot + at + chips, chips)) * 2 + core)

    peers = [device(at) for at in range(1, chips)]
    place = {
        "peers": peers, "me": me, "core": core, "spot": spot, "side": side, "chips": chips, "chip_at": chip_at,
        "right": device(1), "left": device(-1),
        "near": (group, chip * 2 + 1 - core), "twin": (group + 1 - 2 * side, me),
    }
    local = [
        pltpu.make_async_copy(src, dst.at[me], local_sems.at[i])
        for i, (src, dst) in enumerate(((up, u_all), (down, d_all), (weight, w_all)))
    ]
    for copy in local:
        copy.start()

    barrier = pltpu.get_barrier_semaphore()
    greeted = [*peers, place["near"], place["twin"]]
    for to in greeted:
        pl.semaphore_signal(barrier, inc=1, device_id=to, device_id_type=MESH)
    pl.semaphore_wait(barrier, len(greeted))

    sent = []

    def pool(ref, to):
        i = len(sent)
        copy = pltpu.make_async_remote_copy(
            src_ref=ref, dst_ref=ref, send_sem=send_sems.at[i], recv_sem=recv_sems.at[i],
            device_id=to, device_id_type=MESH,
        )
        copy.start()
        sent.append(copy)
        return copy

    ups = Direct(place, pool, u_all)
    downs = Ring(place, pool, d_all, 2, True)
    weights = Ring(place, pool, w_all, 1, True)
    terms = Ring(place, pool, parts, 2, False)
    up_terms = Direct(place, pool, t_all)

    local[0].wait()
    ups.begin()
    local[1].wait()
    downs.begin()
    local[2].wait()
    weights.begin()
    ups.pass_on()
    ups.settle()

    rank, width = down.shape
    outputs = gradient.shape[1]
    tile = 1024
    slot = slot_ref[0]
    up_slot = u_all[slot][:, :outputs]
    back_low = (adapter_scale * dot(gradient[...], up_slot, (1, 1))).astype(BF16)
    back[...] = back_low
    back_turned = back_low.astype(F32).T.astype(BF16)
    mine = stage if staged else parts.at[me]

    @pl.loop(0, width // tile)
    def _(t):
        at = pl.ds(pl.multiple_of(t * tile, tile), tile)
        term = dot(back_turned, hidden[:, at], (1, 0))
        mine[:, at] = term.astype(BF16)
        grad_down[:, at] = jnp.zeros((rank, tile), F32)

    if staged:
        out = pltpu.make_async_copy(stage, parts.at[me], local_sems.at[3])
        out.start()
        out.wait()
    downs.step(1)
    terms.begin()

    def chunk(offset, which):
        return chip_at(lax.rem(spot + offset + chips, chips)) * 2 + which

    def share(j):
        return (u_all[j][0:1, outputs:outputs + 1].astype(F32) == me.astype(F32)).astype(F32)

    def add_terms(i, first):
        j = chunk(i // 2 + first, lax.rem(i, 2))
        weight_of = share(j)
        if staged:
            get = pltpu.make_async_copy(parts.at[j], stage, local_sems.at[3])
            get.start()
            get.wait()

        @pl.loop(0, width // tile)
        def _(t):
            at = pl.ds(pl.multiple_of(t * tile, tile), tile)
            term = stage[:, at] if staged else parts[j, :, at]
            grad_down[:, at] += weight_of * term.astype(F32)

    rows = w_all.shape[1]

    def apply_weight(i, total, first):
        j = chunk(i // 2 + first, lax.rem(i, 2))
        at = pl.ds(pl.multiple_of(j * rows, 128), rows)
        block = w_all[j]
        base = dot(gradient[...], block, (1, 1))
        grad_hidden[:, at] = (base + grad_hidden[:, at].astype(F32)).astype(BF16)
        return total + dot(hidden[:, at], block, (1, 0))

    downs.step(2)
    weights.step(1)
    downs.cross(1)
    for k in range(3, last + 1):
        downs.step(k)
        if k > 3:
            weights.to_twin(k - 2)
        terms.step(k - 2)
        weights.step(k - 1, hold_twin=True)
        downs.cross(k - 1)
        if k > 3:
            weights.cross(k - 3)
    weights.to_twin(last - 1)
    downs.cross(last)
    for k in range(last + 1):
        downs.settle(k)

    def low_part(t, total):
        at = pl.ds(pl.multiple_of(t * tile, tile), tile)
        piece = d_all[slot, :, at]
        grad_hidden[:, at] = dot(back[...], piece, (1, 0)).astype(BF16)
        return total + dot(hidden[:, at], piece, (1, 1))

    low = lax.fori_loop(0, width // tile, low_part, jnp.zeros((hidden.shape[0], rank), F32))
    low_turned = low.astype(BF16).astype(F32).T.astype(BF16)
    t_all[me] = (adapter_scale * dot(low_turned, gradient[...], (1, 0))).astype(BF16)
    up_terms.begin()
    total = adapter_scale * dot(low.astype(BF16), u_all[slot][:, :outputs], (1, 0))

    def use(total, first, offsets):
        total = lax.fori_loop(
            0, 2 * offsets, functools.partial(apply_weight, first=first), total
        )

        @pl.loop(0, 2 * offsets)
        def _(i):
            add_terms(i, first)

        return total

    for k in range(last - 2):
        weights.settle(k)
        terms.settle(k)
    total = use(total, 3 - last, 2 * last - 5)
    terms.step(last - 1)
    weights.cross(last - 2)
    weights.step(last)
    weights.settle(last - 2)
    terms.settle(last - 2)
    total = use(total, last - 2, 1)
    total = use(total, 2 - last, 1)
    terms.step(last)
    up_terms.pass_on()
    weights.cross(last - 1)
    weights.cross(last)
    for k in (last - 1, last):
        weights.settle(k)
        terms.settle(k)
    total = use(total, last - 1, 3)
    values[...] = total.astype(BF16)
    up_terms.settle()
    grad_up[...] = lax.fori_loop(
        0, n, lambda j, held: held + share(j) * t_all[j].astype(F32),
        jnp.zeros(grad_up.shape, F32),
    )
    for copy in sent:
        copy.wait_send()


def ring_order(chips):
    if chips == 8:
        return (
            lambda p: jnp.where(p < 4, 2 * p, 2 * (7 - p) + 1),
            lambda c: jnp.where(lax.rem(c, 2) == 0, c // 2, 7 - c // 2),
        )
    return (lambda p: p, lambda c: c)


def per_device(
    hidden,
    output_gradient,
    frozen_value_weight,
    adapter_down_maps,
    adapter_up_maps,
    owner,
    token_block_tenant,
):
    n = lax.axis_size("fsdp")
    chips = n // 2
    rows, width = hidden.shape
    outputs = output_gradient.shape[1]
    rank = adapter_down_maps.shape[2]
    tenants = owner.shape[0]
    staged = n > 16
    slot = jnp.sum(
        jnp.where(token_block_tenant[0, 0] == jnp.arange(tenants, dtype=jnp.int32), owner, 0)
    )
    up = jnp.concatenate(
        [adapter_up_maps[0], jnp.broadcast_to(slot.astype(BF16), (rank, 128))], axis=1
    )
    down = adapter_down_maps[0].T
    count = 2 * copies_of(chips, True) + copies_of(chips, False) + 2 * (2 * chips - 1)
    vmem = pl.BlockSpec(memory_space=pltpu.VMEM)
    hbm = pl.BlockSpec(memory_space=pl.ANY)
    out_shape = [
        jax.ShapeDtypeStruct((rows, outputs), BF16),
        jax.ShapeDtypeStruct((rows, width), BF16),
        jax.ShapeDtypeStruct((rank, width), F32),
        jax.ShapeDtypeStruct((rank, outputs), F32),
    ]
    out_specs = [vmem] * 4
    scratch = []
    if staged:
        out_shape.append(jax.ShapeDtypeStruct((n, rank, width), BF16))
        out_specs.append(hbm)
    else:
        scratch.append(pltpu.VMEM((n, rank, width), BF16))
    scratch += [
        pltpu.VMEM((n,) + frozen_value_weight.shape, BF16),
        pltpu.VMEM((n, rank, width), BF16),
        pltpu.VMEM((n,) + up.shape, BF16),
        pltpu.VMEM((n, rank, outputs), BF16),
        pltpu.VMEM((rows, rank), BF16),
    ]
    if staged:
        scratch.append(pltpu.VMEM((rank, width), BF16))
    scratch += [
        pltpu.SemaphoreType.DMA((count,)),
        pltpu.SemaphoreType.DMA((count,)),
        pltpu.SemaphoreType.DMA((4,)),
    ]
    results = pl.pallas_call(
        functools.partial(kernel, n, ring_order(chips), staged),
        out_shape=out_shape,
        in_specs=[pl.BlockSpec(memory_space=pltpu.SMEM), vmem, vmem, hbm, hbm, hbm],
        out_specs=out_specs,
        scratch_shapes=scratch,
        compiler_params=pltpu.CompilerParams(
            collective_id=0, has_side_effects=True, vmem_limit_bytes=56 << 20
        ),
    )(slot.reshape(1), hidden, output_gradient, frozen_value_weight, down, up)
    values, grad_hidden, grad_down, grad_up = results[:4]
    return values, grad_hidden, grad_down.T[None], grad_up[None]


def solution(mesh):
    return jax.shard_map(
        per_device,
        mesh=mesh,
        in_specs=(
            P(("groups", "fsdp"), None),
            P(("groups", "fsdp"), None),
            P("fsdp", None),
            P("fsdp", None, None),
            P("fsdp", None, None),
            P(),
            P(("groups", "fsdp"), None),
        ),
        out_specs=(
            P(("groups", "fsdp"), None),
            P(("groups", "fsdp"), None),
            P(("groups", "fsdp"), None, None),
            P(("groups", "fsdp"), None, None),
        ),
        check_vma=False,
    )
```

```python
import functools

import jax
import jax.numpy as jnp
from jax import lax
from jax.experimental import pallas as pl
from jax.experimental.pallas import tpu as pltpu
from jax.sharding import PartitionSpec as P

MESH = pl.DeviceIdType.MESH
adapter_scale = 2.0
F32 = jnp.float32
BF16 = jnp.bfloat16


def dot(a, b, over):
    return lax.dot_general(a, b, ((over[:1], over[1:]), ((), ())), preferred_element_type=F32)


class Ring:
    def __init__(self, place, pool, buf, axis, shared):
        self.place, self.pool, self.buf, self.axis = place, pool, buf, axis
        length = buf.shape[axis]
        self.shared = shared
        unit = 32 if axis == 1 else 256
        self.length = max(length // 2, length * 9 // 16 // unit * unit) if shared else length
        self.swapped = length - self.length
        self.start_at = place["side"] * self.swapped if shared else 0
        self.out_at = place["side"] * self.length if shared else 0
        self.other_at = (1 - place["side"]) * self.length if shared else 0
        self.right, self.left, self.twin, self.near = {}, {}, {}, {}
        self.near_twin = {}

    def view(self, index, start, length):
        if self.axis == 1:
            return self.buf.at[index, pl.ds(pl.multiple_of(start, 16), length), :]
        return self.buf.at[index, :, pl.ds(pl.multiple_of(start, 128), length)]

    def send(self, index, start, length, to):
        ref = self.view(index, start, length)
        return self.pool(ref, to)

    def chip(self, offset):
        place = self.place
        return place["chip_at"](lax.rem(place["spot"] + offset + place["chips"], place["chips"]))

    def mine(self, offset):
        return self.chip(offset) * 2 + self.place["core"]

    def begin(self):
        place = self.place
        self.near[0] = [self.send(place["me"], 0, self.buf.shape[self.axis], place["near"])]
        self.right[1] = self.send(place["me"], self.start_at, self.length, place["right"])
        self.left[1] = self.send(place["me"], self.start_at, self.length, place["left"])

    def step(self, k, hold_twin=False):
        place, half = self.place, self.length // 2
        last = place["chips"] // 2
        from_left, from_right = self.mine(-k), self.mine(k)
        self.right[k].wait_recv()
        if k + 1 <= last:
            size = self.length if k + 1 < last else half
            self.right[k + 1] = self.send(from_left, self.start_at, size, place["right"])
        self.left[k].wait_recv()
        if k + 1 <= last:
            size = self.length if k + 1 < last else half
            self.left[k + 1] = self.send(
                from_right, self.start_at + self.length - size, size, place["left"]
            )
        got = [from_left, from_right] if k < last else [from_left]
        if self.shared and not hold_twin:
            self.to_twin(k)
        self.near[k] = [self.send(i, self.start_at, self.length, place["near"]) for i in got]

    def got(self, k):
        return [self.mine(-k), self.mine(k)] if k < self.place["chips"] // 2 else [self.mine(-k)]

    def to_twin(self, k):
        to = self.place["twin"]
        self.twin[k] = [self.send(i, self.out_at, self.swapped, to) for i in self.got(k)]

    def cross(self, k):
        place, got = self.place, self.got(k)
        self.near_twin[k] = []
        for i, copy in zip(got, self.twin[k]):
            copy.wait_recv()
            self.near_twin[k].append(self.send(i, self.other_at, self.swapped, place["near"]))

    def settle(self, k):
        for copy in self.near[k]:
            copy.wait_recv()
        for copy in self.near_twin.get(k, []):
            copy.wait_recv()


class Lanes:
    def __init__(self, place, make, parts, sums_in, sums_out, cross_in, cross_out):
        core, chip = place["core"], place["chip"]
        self.place, self.parts = place, parts
        self.sums_in, self.sums_out = sums_in, sums_out
        self.cross_in, self.cross_out = cross_in, cross_out
        group, me = place["group"], place["me"]
        z, y = chip // 2, lax.rem(chip, 2)
        self.z, self.y = z, y
        self.inner = (z == 1) | (z == 2)
        self.outer = jnp.logical_not(self.inner)
        self.z_out = jnp.where(z < 2, 0, 3)
        z_in = jnp.where(self.inner, 3 - z, jnp.where(z == 0, 1, 2))

        def at(where_z, where_y, which):
            return (where_z * 2 + where_y) * 2 + which

        self.at = at
        inward, outward = (group, at(z_in, y, core)), (group, at(self.z_out, y, core))
        near, across = place["near"], (group, at(z, 1 - y, core))

        def block(j, to):
            return make(parts.at[j], parts.at[j], to)

        behind, facing = at(self.z_out, y, core), at(3 - z, y, core)
        far = at(3 - self.z_out, y, core)
        self.own_near = block(me, near)
        self.first, self.second = block(me, inward), block(me, inward)
        self.relay = block(behind, inward)
        self.near = [block(j, near) for j in (behind, facing, far)]
        self.sums = [make(sums_out.at[i], sums_in.at[i], outward) for i in range(2)]
        self.cross = make(cross_out, cross_in, across)

    def begin(self):
        self.own_near.start()

        @pl.when(self.outer)
        def _():
            self.first.start()

        @pl.when(self.inner)
        def _():
            self.second.start()

    def relay_on(self):
        @pl.when(self.inner)
        def _():
            self.first.wait_recv()
            self.relay.start()
            self.near[0].start()

    def facing_in(self):
        @pl.when(self.inner)
        def _():
            self.second.wait_recv()
            self.near[1].start()

    def far_in(self):
        @pl.when(self.inner)
        def _():
            self.relay.wait_recv()
            self.near[2].start()

    def over_tiles(self, body):
        width, tile = self.parts.shape[2], 1024

        @pl.loop(0, width // tile)
        def _(t):
            body(pl.ds(pl.multiple_of(t * tile, tile), tile))

    def add(self, blocks, share, slots):
        weights = [[share(j, slot) for j in blocks] for slot in slots]

        def at_tile(at):
            terms = [self.parts[j, :, at].astype(F32) for j in blocks]
            return [sum(w * term for w, term in zip(row, terms)) for row in weights]

        return at_tile

    def sum_inner(self, share, mine_ref):
        place, at = self.place, self.at
        me, core = place["me"], place["core"]
        z, y = self.z, self.y

        @pl.when(self.inner)
        def _():
            self.own_near.wait_recv()
            for copy in self.near:
                copy.wait_recv()
            rest = [at(q, y, c) for q in (z, 3 - z, 3 - self.z_out) for c in (0, 1)]
            outward = self.add(rest, share, [at(self.z_out, i, core) for i in (0, 1)])

            def body(tile):
                for i, total in enumerate(outward(tile)):
                    self.sums_out[i, :, tile] = total.astype(BF16)

            self.over_tiles(body)
            for copy in self.sums:
                copy.start()
            row = [at(q, y, c) for q in range(4) for c in (0, 1)]
            column = self.add(row, share, [me, at(z, 1 - y, core)])

            def body(tile):
                held, other = column(tile)
                mine_ref[:, tile] = held
                self.cross_out[:, tile] = other.astype(BF16)

            self.over_tiles(body)
            self.cross.start()

    def sum_outer(self, share, mine_ref):
        place, at = self.place, self.at
        me, core = place["me"], place["core"]
        z, y = self.z, self.y

        @pl.when(self.outer)
        def _():
            self.own_near.wait_recv()
            for copy in self.sums:
                copy.wait_recv()
            column = self.add([at(z, y, c) for c in (0, 1)], share, [me, at(z, 1 - y, core)])

            def body(tile):
                held, other = column(tile)
                mine_ref[:, tile] = held + self.sums_in[y, :, tile].astype(F32)
                other = other + self.sums_in[1 - y, :, tile].astype(F32)
                self.cross_out[:, tile] = other.astype(BF16)

            self.over_tiles(body)
            self.cross.start()

    def finish(self, mine_ref):
        self.cross.wait_recv()

        def body(tile):
            mine_ref[:, tile] += self.cross_in[:, tile].astype(F32)

        self.over_tiles(body)

    def drain(self):
        self.own_near.wait_send()
        self.cross.wait_send()

        @pl.when(self.outer)
        def _():
            self.first.wait_send()

        @pl.when(self.inner)
        def _():
            for copy in (self.second, self.relay, *self.near, *self.sums):
                copy.wait_send()


class Direct:
    def __init__(self, place, pool, buf):
        self.place, self.pool, self.buf = place, pool, buf

    def begin(self):
        place = self.place
        ref = self.buf.at[place["me"]]
        self.far = [self.pool(ref, to) for to in place["peers"]]
        self.near = [self.pool(ref, place["near"])]

    def pass_on(self):
        chips = self.place["chips"]
        for offset, copy in enumerate(self.far, 1):
            copy.wait_recv()
            spot = lax.rem(self.place["spot"] - offset + chips, chips)
            ref = self.buf.at[self.place["chip_at"](spot) * 2 + self.place["core"]]
            self.near.append(self.pool(ref, self.place["near"]))

    def settle(self):
        for copy in self.near:
            copy.wait_recv()


def copies_of(chips, shared):
    last = chips // 2
    got = 2 * last - 1
    return 1 + 2 * last + got * (3 if shared else 1)


def kernel(
    n, ring_of, staged,
    owner, tenant, hidden, gradient, weight, down, up,
    values, grad_hidden, grad_down, grad_up, *rest,
):
    lanes_used = n == 16
    parts, w_all, d_all, u_all, t_all, back = rest[:6]
    send_sems, recv_sems, local_sems = rest[-3:]
    stage = rest[6] if staged else None
    me = lax.axis_index("fsdp")
    group = lax.axis_index("groups")
    chips, last = n // 2, n // 4
    core, chip = lax.rem(me, 2), me // 2
    chip_at, spot_of = ring_of
    spot = spot_of(chip)
    side = lax.rem(group, 2)

    def device(at):
        return (group, chip_at(lax.rem(spot + at + chips, chips)) * 2 + core)

    peers = [device(at) for at in range(1, chips)]
    place = {
        "peers": peers, "me": me, "group": group, "chip": chip, "core": core, "spot": spot, "side": side, "chips": chips, "chip_at": chip_at,
        "right": device(1), "left": device(-1),
        "near": (group, chip * 2 + 1 - core), "twin": (group + 1 - 2 * side, me),
    }
    local = [
        pltpu.make_async_copy(src, dst.at[me], local_sems.at[i])
        for i, (src, dst) in enumerate(((down, d_all), (weight, w_all)))
    ]
    for copy in local:
        copy.start()

    slot = jnp.int32(0)
    for t in range(owner.shape[0]):
        slot = slot + jnp.where(tenant[0, 0] == t, owner[t], 0)
    rank, width = down.shape
    outputs = gradient.shape[1]
    u_all[me, :, :outputs] = up[...]
    u_all[me, :, outputs:] = jnp.broadcast_to(slot.astype(F32), (rank, 128)).astype(BF16)

    barrier = pltpu.get_barrier_semaphore()
    greeted = [*peers, place["near"], place["twin"]]
    for to in greeted:
        pl.semaphore_signal(barrier, inc=1, device_id=to, device_id_type=MESH)
    pl.semaphore_wait(barrier, len(greeted))

    sent = []

    made = []

    def make(src, dst, to):
        i = len(made)
        made.append(i)
        return pltpu.make_async_remote_copy(
            src_ref=src, dst_ref=dst, send_sem=send_sems.at[i], recv_sem=recv_sems.at[i],
            device_id=to, device_id_type=MESH,
        )

    def pool(ref, to):
        copy = make(ref, ref, to)
        copy.start()
        sent.append(copy)
        return copy

    ups = Direct(place, pool, u_all)
    downs = Ring(place, pool, d_all, 2, True)
    weights = Ring(place, pool, w_all, 1, True)
    if lanes_used:
        terms = Lanes(place, make, parts, *rest[6:10])
    else:
        terms = Ring(place, pool, parts, 2, False)
    up_terms = Direct(place, pool, t_all)

    ups.begin()
    local[0].wait()
    downs.begin()
    local[1].wait()
    weights.begin()
    ups.pass_on()
    ups.settle()

    tile = 1024
    up_slot = u_all[slot][:, :outputs]
    back_low = (adapter_scale * dot(gradient[...], up_slot, (1, 1))).astype(BF16)
    back[...] = back_low
    back_turned = back_low.astype(F32).T.astype(BF16)
    mine = stage if staged else parts.at[me]

    @pl.loop(0, width // tile)
    def _(t):
        at = pl.ds(pl.multiple_of(t * tile, tile), tile)
        term = dot(back_turned, hidden[:, at], (1, 0))
        mine[:, at] = term.astype(BF16)
        grad_down[:, at] = jnp.zeros((rank, tile), F32)

    if staged:
        out = pltpu.make_async_copy(stage, parts.at[me], local_sems.at[3])
        out.start()
        out.wait()
    downs.step(1)
    terms.begin()

    def chunk(offset, which):
        return chip_at(lax.rem(spot + offset + chips, chips)) * 2 + which

    def share(j, to=me):
        return (u_all[j][0:1, outputs:outputs + 1].astype(F32) == to.astype(F32)).astype(F32)

    def add_terms(i, first):
        j = chunk(i // 2 + first, lax.rem(i, 2))
        weight_of = share(j)
        if staged:
            get = pltpu.make_async_copy(parts.at[j], stage, local_sems.at[3])
            get.start()
            get.wait()

        @pl.loop(0, width // tile)
        def _(t):
            at = pl.ds(pl.multiple_of(t * tile, tile), tile)
            term = stage[:, at] if staged else parts[j, :, at]
            grad_down[:, at] += weight_of * term.astype(F32)

    rows = w_all.shape[1]

    def apply_weight(i, total, first):
        j = chunk(i // 2 + first, lax.rem(i, 2))
        at = pl.ds(pl.multiple_of(j * rows, 128), rows)
        block = w_all[j]
        base = dot(gradient[...], block, (1, 1))
        grad_hidden[:, at] = (base + grad_hidden[:, at].astype(F32)).astype(BF16)
        return total + dot(hidden[:, at], block, (1, 0))

    downs.step(2)
    weights.step(1)
    downs.cross(1)
    for k in range(3, last + 1):
        downs.step(k)
        if k > 3:
            weights.to_twin(k - 2)
        if not lanes_used:
            terms.step(k - 2)
        elif k == 3:
            terms.relay_on()
        else:
            terms.facing_in()
        weights.step(k - 1, hold_twin=True)
        downs.cross(k - 1)
        if k > 3:
            weights.cross(k - 3)
    weights.to_twin(last - 1)
    downs.cross(last)
    for k in range(last + 1):
        downs.settle(k)

    def low_part(t, total):
        at = pl.ds(pl.multiple_of(t * tile, tile), tile)
        piece = d_all[slot, :, at]
        grad_hidden[:, at] = dot(back[...], piece, (1, 0)).astype(BF16)
        return total + dot(hidden[:, at], piece, (1, 1))

    low = lax.fori_loop(0, width // tile, low_part, jnp.zeros((hidden.shape[0], rank), F32))
    low_turned = low.astype(BF16).astype(F32).T.astype(BF16)
    t_all[me] = (adapter_scale * dot(low_turned, gradient[...], (1, 0))).astype(BF16)
    up_terms.begin()
    total = adapter_scale * dot(low.astype(BF16), u_all[slot][:, :outputs], (1, 0))

    def use(total, first, offsets):
        total = lax.fori_loop(
            0, 2 * offsets, functools.partial(apply_weight, first=first), total
        )

        if not lanes_used:

            @pl.loop(0, 2 * offsets)
            def _(i):
                add_terms(i, first)

        return total

    for k in range(last - 2):
        weights.settle(k)
        if not lanes_used:
            terms.settle(k)
    if lanes_used:
        terms.far_in()
        terms.sum_inner(share, grad_down)
    total = use(total, 3 - last, 2 * last - 5)
    if not lanes_used:
        terms.step(last - 1)
    weights.cross(last - 2)
    weights.step(last)
    weights.settle(last - 2)
    if not lanes_used:
        terms.settle(last - 2)
    total = use(total, last - 2, 1)
    total = use(total, 2 - last, 1)
    if lanes_used:
        terms.sum_outer(share, grad_down)
    else:
        terms.step(last)
    up_terms.pass_on()
    weights.cross(last - 1)
    weights.cross(last)
    for k in (last - 1, last):
        weights.settle(k)
        if not lanes_used:
            terms.settle(k)
    total = use(total, last - 1, 3)
    values[...] = total.astype(BF16)
    up_terms.settle()
    grad_up[...] = lax.fori_loop(
        0, n, lambda j, held: held + share(j) * t_all[j].astype(F32),
        jnp.zeros(grad_up.shape, F32),
    )
    if lanes_used:
        terms.finish(grad_down)
        terms.drain()
    for copy in sent:
        copy.wait_send()


def ring_order(chips):
    if chips == 8:
        return (
            lambda p: jnp.where(p < 4, 2 * p, 2 * (7 - p) + 1),
            lambda c: jnp.where(lax.rem(c, 2) == 0, c // 2, 7 - c // 2),
        )
    return (lambda p: p, lambda c: c)


def per_device(
    hidden,
    output_gradient,
    frozen_value_weight,
    adapter_down_maps,
    adapter_up_maps,
    owner,
    token_block_tenant,
):
    n = lax.axis_size("fsdp")
    chips = n // 2
    rows, width = hidden.shape
    outputs = output_gradient.shape[1]
    rank = adapter_down_maps.shape[2]
    staged = n > 16
    down = adapter_down_maps[0].T
    count = 2 * copies_of(chips, True) + copies_of(chips, False) + 2 * (2 * chips - 1)
    vmem = pl.BlockSpec(memory_space=pltpu.VMEM)
    smem = pl.BlockSpec(memory_space=pltpu.SMEM)
    hbm = pl.BlockSpec(memory_space=pl.ANY)
    out_shape = [
        jax.ShapeDtypeStruct((rows, outputs), BF16),
        jax.ShapeDtypeStruct((rows, width), BF16),
        jax.ShapeDtypeStruct((rank, width), F32),
        jax.ShapeDtypeStruct((rank, outputs), F32),
    ]
    out_specs = [vmem] * 4
    scratch = []
    if staged:
        out_shape.append(jax.ShapeDtypeStruct((n, rank, width), BF16))
        out_specs.append(hbm)
    else:
        scratch.append(pltpu.VMEM((n, rank, width), BF16))
    scratch += [
        pltpu.VMEM((n,) + frozen_value_weight.shape, BF16),
        pltpu.VMEM((n, rank, width), BF16),
        pltpu.VMEM((n, rank, outputs + 128), BF16),
        pltpu.VMEM((n, rank, outputs), BF16),
        pltpu.VMEM((rows, rank), BF16),
    ]
    if staged:
        scratch.append(pltpu.VMEM((rank, width), BF16))
    elif n == 16:
        pair, single = pltpu.VMEM((2, rank, width), BF16), pltpu.VMEM((rank, width), BF16)
        scratch += [pair, pair, single, single]
    scratch += [
        pltpu.SemaphoreType.DMA((count,)),
        pltpu.SemaphoreType.DMA((count,)),
        pltpu.SemaphoreType.DMA((4,)),
    ]
    results = pl.pallas_call(
        functools.partial(kernel, n, ring_order(chips), staged),
        out_shape=out_shape,
        in_specs=[smem, smem, vmem, vmem, hbm, hbm, vmem],
        out_specs=out_specs,
        scratch_shapes=scratch,
        compiler_params=pltpu.CompilerParams(
            collective_id=0, has_side_effects=True, vmem_limit_bytes=56 << 20
        ),
    )(
        owner, token_block_tenant, hidden, output_gradient, frozen_value_weight, down,
        adapter_up_maps[0],
    )
    values, grad_hidden, grad_down, grad_up = results[:4]
    return values, grad_hidden, grad_down.T[None], grad_up[None]


def solution(mesh):
    return jax.shard_map(
        per_device,
        mesh=mesh,
        in_specs=(
            P(("groups", "fsdp"), None),
            P(("groups", "fsdp"), None),
            P("fsdp", None),
            P("fsdp", None, None),
            P("fsdp", None, None),
            P(),
            P(("groups", "fsdp"), None),
        ),
        out_specs=(
            P(("groups", "fsdp"), None),
            P(("groups", "fsdp"), None),
            P(("groups", "fsdp"), None, None),
            P(("groups", "fsdp"), None, None),
        ),
        check_vma=False,
    )
```

```python
import functools

import jax
import jax.numpy as jnp
from jax import lax
from jax.experimental import pallas as pl
from jax.experimental.pallas import tpu as pltpu
from jax.sharding import PartitionSpec as P

MESH = pl.DeviceIdType.MESH
adapter_scale = 2.0
F32 = jnp.float32
BF16 = jnp.bfloat16


def dot(a, b, over):
    return lax.dot_general(a, b, ((over[:1], over[1:]), ((), ())), preferred_element_type=F32)


class Ring:
    def __init__(self, place, pool, buf, axis, shared):
        self.place, self.pool, self.buf, self.axis = place, pool, buf, axis
        length = buf.shape[axis]
        self.shared = shared
        self.length = length // 2 if shared else length
        self.start_at = place["side"] * self.length if shared else 0
        self.other_at = (1 - place["side"]) * self.length if shared else 0
        self.right, self.left, self.twin, self.near = {}, {}, {}, {}
        self.near_twin = {}

    def view(self, index, start, length):
        if self.axis == 1:
            return self.buf.at[index, pl.ds(pl.multiple_of(start, 16), length), :]
        return self.buf.at[index, :, pl.ds(pl.multiple_of(start, 128), length)]

    def send(self, index, start, length, to, only=None):
        ref = self.view(index, start, length)
        return self.pool(ref, to, only)

    def chip(self, offset):
        place = self.place
        return place["chip_at"](lax.rem(place["spot"] + offset + place["chips"], place["chips"]))

    def mine(self, offset):
        return self.chip(offset) * 2 + self.place["core"]

    def begin(self):
        place = self.place
        self.near[0] = [self.send(place["me"], 0, self.buf.shape[self.axis], place["near"])]
        self.right[1] = self.send(place["me"], self.start_at, self.length, place["right"])
        self.left[1] = self.send(place["me"], self.start_at, self.length, place["left"])

    def step(self, k, hold_twin=False):
        place, half = self.place, self.length // 2
        last, short = place["chips"] // 2, place["short"]
        from_left, from_right = self.mine(-k), self.mine(k)

        def onward(spot, index, offset, to):
            if k + 1 < last:
                return self.send(index, self.start_at, self.length, to)
            only = jnp.logical_not(place["inner"](spot)) if short else None
            return self.send(index, self.start_at + offset, half, to, only)

        def arrive(copy):
            if k == last and short:
                pl.when(jnp.logical_not(place["inner"](0)))(copy.wait_recv)
            else:
                copy.wait_recv()

        arrive(self.right[k])
        if k < last:
            self.right[k + 1] = onward(1, from_left, 0, place["right"])
        arrive(self.left[k])
        if k < last:
            self.left[k + 1] = onward(-1, from_right, self.length - half, place["left"])
        if short and k == 1:
            self.across = self.send(
                place["facing"], self.start_at, self.length, place["across"], place["inner"](0)
            )
        if short and k == last:
            pl.when(place["inner"](0))(self.across.wait_recv)
        got = self.got(k)
        if self.shared and not hold_twin:
            self.to_twin(k)
        self.near[k] = [self.send(i, self.start_at, self.length, place["near"]) for i in got]

    def got(self, k):
        return [self.mine(-k), self.mine(k)] if k < self.place["chips"] // 2 else [self.mine(-k)]

    def to_twin(self, k):
        to = self.place["twin"]
        self.twin[k] = [self.send(i, self.start_at, self.length, to) for i in self.got(k)]

    def cross(self, k):
        place, got = self.place, self.got(k)
        self.near_twin[k] = []
        for i, copy in zip(got, self.twin[k]):
            copy.wait_recv()
            self.near_twin[k].append(self.send(i, self.other_at, self.length, place["near"]))

    def settle(self, k):
        for copy in self.near[k]:
            copy.wait_recv()
        for copy in self.near_twin.get(k, []):
            copy.wait_recv()


class Direct:
    def __init__(self, place, pool, buf):
        self.place, self.pool, self.buf = place, pool, buf

    def begin(self):
        place = self.place
        ref = self.buf.at[place["me"]]
        self.far = [self.pool(ref, to) for to in place["peers"]]
        self.near = [self.pool(ref, place["near"])]

    def pass_on(self):
        chips = self.place["chips"]
        for offset, copy in enumerate(self.far, 1):
            copy.wait_recv()
            spot = lax.rem(self.place["spot"] - offset + chips, chips)
            ref = self.buf.at[self.place["chip_at"](spot) * 2 + self.place["core"]]
            self.near.append(self.pool(ref, self.place["near"]))

    def settle(self):
        for copy in self.near:
            copy.wait_recv()


def copies_of(chips, shared):
    last = chips // 2
    got = 2 * last - 1
    return 2 + 2 * last + got * (3 if shared else 1)


def kernel(
    n, ring_of, staged,
    owner, tenant, hidden, gradient, weight, down, up,
    values, grad_hidden, grad_down, grad_up, *rest,
):
    if staged:
        parts, w_all, d_all, u_all, t_all, back, stage, send_sems, recv_sems, local_sems = rest
    else:
        parts, w_all, d_all, u_all, t_all, back, send_sems, recv_sems, local_sems = rest
    me = lax.axis_index("fsdp")
    group = lax.axis_index("groups")
    chips, last = n // 2, n // 4
    core, chip = lax.rem(me, 2), me // 2
    chip_at, spot_of = ring_of
    spot = spot_of(chip)
    side = lax.rem(group, 2)

    def device(at):
        return (group, chip_at(lax.rem(spot + at + chips, chips)) * 2 + core)

    peers = [device(at) for at in range(1, chips)]
    short = chips == 8

    def inner(at):
        z = chip_at(lax.rem(spot + at + chips, chips)) // 2
        return (z == 1) | (z == 2)

    facing = (3 - chip // 2) * 4 + lax.rem(chip, 2) * 2 + core
    place = {
        "short": short, "inner": inner, "facing": facing,
        "across": (group, me + 2 - 4 * lax.rem(chip, 2)),
        "peers": peers, "me": me, "core": core, "spot": spot, "side": side, "chips": chips, "chip_at": chip_at,
        "right": device(1), "left": device(-1),
        "near": (group, chip * 2 + 1 - core), "twin": (group + 1 - 2 * side, me),
    }
    local = [
        pltpu.make_async_copy(src, dst.at[me], local_sems.at[i])
        for i, (src, dst) in enumerate(((down, d_all), (weight, w_all)))
    ]
    for copy in local:
        copy.start()

    slot = jnp.int32(0)
    for t in range(owner.shape[0]):
        slot = slot + jnp.where(tenant[0, 0] == t, owner[t], 0)
    rank, width = down.shape
    outputs = gradient.shape[1]
    u_all[me, :, :outputs] = up[...]
    u_all[me, :, outputs:] = jnp.broadcast_to(slot.astype(F32), (rank, 128)).astype(BF16)

    barrier = pltpu.get_barrier_semaphore()
    greeted = [*peers, place["near"], place["twin"]]
    for to in greeted:
        pl.semaphore_signal(barrier, inc=1, device_id=to, device_id_type=MESH)
    pl.semaphore_wait(barrier, len(greeted))

    sent = []

    maybe = []

    def pool(ref, to, only=None):
        i = len(sent) + len(maybe)
        copy = pltpu.make_async_remote_copy(
            src_ref=ref, dst_ref=ref, send_sem=send_sems.at[i], recv_sem=recv_sems.at[i],
            device_id=to, device_id_type=MESH,
        )
        if only is None:
            copy.start()
            sent.append(copy)
        else:
            maybe.append((only, copy))
            pl.when(only)(copy.start)
        return copy

    ups = Direct(place, pool, u_all)
    downs = Ring(place, pool, d_all, 2, True)
    weights = Ring(place, pool, w_all, 1, True)
    terms = Ring(place, pool, parts, 2, False)
    up_terms = Direct(place, pool, t_all)

    local[0].wait()
    downs.begin()
    ups.begin()
    local[1].wait()
    weights.begin()
    downs.step(1)
    ups.pass_on()
    ups.settle()

    tile = 1024
    up_slot = u_all[slot][:, :outputs]
    back_low = (adapter_scale * dot(gradient[...], up_slot, (1, 1))).astype(BF16)
    back[...] = back_low
    back_turned = back_low.astype(F32).T.astype(BF16)
    mine = stage if staged else parts.at[me]

    @pl.loop(0, width // tile)
    def _(t):
        at = pl.ds(pl.multiple_of(t * tile, tile), tile)
        term = dot(back_turned, hidden[:, at], (1, 0))
        mine[:, at] = term.astype(BF16)
        grad_down[:, at] = jnp.zeros((rank, tile), F32)

    if staged:
        out = pltpu.make_async_copy(stage, parts.at[me], local_sems.at[3])
        out.start()
        out.wait()
    terms.begin()

    def chunk(offset, which):
        return chip_at(lax.rem(spot + offset + chips, chips)) * 2 + which

    def share(j):
        return (u_all[j][0:1, outputs:outputs + 1].astype(F32) == me.astype(F32)).astype(F32)

    def add_terms(i, first):
        j = chunk(i // 2 + first, lax.rem(i, 2))
        weight_of = share(j)
        if staged:
            get = pltpu.make_async_copy(parts.at[j], stage, local_sems.at[3])
            get.start()
            get.wait()

        @pl.loop(0, width // tile)
        def _(t):
            at = pl.ds(pl.multiple_of(t * tile, tile), tile)
            term = stage[:, at] if staged else parts[j, :, at]
            grad_down[:, at] += weight_of * term.astype(F32)

    rows = w_all.shape[1]

    def apply_weight(i, total, first):
        j = chunk(i // 2 + first, lax.rem(i, 2))
        at = pl.ds(pl.multiple_of(j * rows, 128), rows)
        block = w_all[j]
        base = dot(gradient[...], block, (1, 1))
        grad_hidden[:, at] = (base + grad_hidden[:, at].astype(F32)).astype(BF16)
        return total + dot(hidden[:, at], block, (1, 0))

    downs.step(2)
    weights.step(1)
    downs.cross(1)
    for k in range(3, last + 1):
        downs.step(k)
        if k > 3:
            weights.to_twin(k - 2)
        terms.step(k - 2)
        weights.step(k - 1, hold_twin=True)
        downs.cross(k - 1)
        if k > 3:
            weights.cross(k - 3)
    weights.to_twin(last - 1)
    downs.cross(last)
    for k in range(last + 1):
        downs.settle(k)

    def low_part(t, total):
        at = pl.ds(pl.multiple_of(t * tile, tile), tile)
        piece = d_all[slot, :, at]
        grad_hidden[:, at] = dot(back[...], piece, (1, 0)).astype(BF16)
        return total + dot(hidden[:, at], piece, (1, 1))

    low = lax.fori_loop(0, width // tile, low_part, jnp.zeros((hidden.shape[0], rank), F32))
    low_turned = low.astype(BF16).astype(F32).T.astype(BF16)
    t_all[me] = (adapter_scale * dot(low_turned, gradient[...], (1, 0))).astype(BF16)
    up_terms.begin()
    total = adapter_scale * dot(low.astype(BF16), u_all[slot][:, :outputs], (1, 0))

    def use(total, first, offsets):
        total = lax.fori_loop(
            0, 2 * offsets, functools.partial(apply_weight, first=first), total
        )

        @pl.loop(0, 2 * offsets)
        def _(i):
            add_terms(i, first)

        return total

    for k in range(last - 2):
        weights.settle(k)
        terms.settle(k)
    total = use(total, 3 - last, 2 * last - 5)
    terms.step(last - 1)
    weights.cross(last - 2)
    weights.step(last)
    weights.settle(last - 2)
    terms.settle(last - 2)
    total = use(total, last - 2, 1)
    total = use(total, 2 - last, 1)
    terms.step(last)
    up_terms.pass_on()
    weights.cross(last - 1)
    weights.cross(last)
    for k in (last - 1, last):
        weights.settle(k)
        terms.settle(k)
    total = use(total, last - 1, 3)
    values[...] = total.astype(BF16)
    up_terms.settle()
    grad_up[...] = lax.fori_loop(
        0, n, lambda j, held: held + share(j) * t_all[j].astype(F32),
        jnp.zeros(grad_up.shape, F32),
    )
    for copy in sent:
        copy.wait_send()
    for only, copy in maybe:
        pl.when(only)(copy.wait_send)


def ring_order(chips):
    if chips == 8:
        return (
            lambda p: jnp.where(p < 4, 2 * p, 2 * (7 - p) + 1),
            lambda c: jnp.where(lax.rem(c, 2) == 0, c // 2, 7 - c // 2),
        )
    return (lambda p: p, lambda c: c)


def per_device(
    hidden,
    output_gradient,
    frozen_value_weight,
    adapter_down_maps,
    adapter_up_maps,
    owner,
    token_block_tenant,
):
    n = lax.axis_size("fsdp")
    chips = n // 2
    rows, width = hidden.shape
    outputs = output_gradient.shape[1]
    rank = adapter_down_maps.shape[2]
    staged = n > 16
    down = adapter_down_maps[0].T
    count = 2 * copies_of(chips, True) + copies_of(chips, False) + 2 * (2 * chips - 1)
    vmem = pl.BlockSpec(memory_space=pltpu.VMEM)
    smem = pl.BlockSpec(memory_space=pltpu.SMEM)
    hbm = pl.BlockSpec(memory_space=pl.ANY)
    out_shape = [
        jax.ShapeDtypeStruct((rows, outputs), BF16),
        jax.ShapeDtypeStruct((rows, width), BF16),
        jax.ShapeDtypeStruct((rank, width), F32),
        jax.ShapeDtypeStruct((rank, outputs), F32),
    ]
    out_specs = [vmem] * 4
    scratch = []
    if staged:
        out_shape.append(jax.ShapeDtypeStruct((n, rank, width), BF16))
        out_specs.append(hbm)
    else:
        scratch.append(pltpu.VMEM((n, rank, width), BF16))
    scratch += [
        pltpu.VMEM((n,) + frozen_value_weight.shape, BF16),
        pltpu.VMEM((n, rank, width), BF16),
        pltpu.VMEM((n, rank, outputs + 128), BF16),
        pltpu.VMEM((n, rank, outputs), BF16),
        pltpu.VMEM((rows, rank), BF16),
    ]
    if staged:
        scratch.append(pltpu.VMEM((rank, width), BF16))
    scratch += [
        pltpu.SemaphoreType.DMA((count,)),
        pltpu.SemaphoreType.DMA((count,)),
        pltpu.SemaphoreType.DMA((4,)),
    ]
    results = pl.pallas_call(
        functools.partial(kernel, n, ring_order(chips), staged),
        out_shape=out_shape,
        in_specs=[smem, smem, vmem, vmem, hbm, hbm, vmem],
        out_specs=out_specs,
        scratch_shapes=scratch,
        compiler_params=pltpu.CompilerParams(
            collective_id=0, has_side_effects=True, vmem_limit_bytes=56 << 20
        ),
    )(
        owner, token_block_tenant, hidden, output_gradient, frozen_value_weight, down,
        adapter_up_maps[0],
    )
    values, grad_hidden, grad_down, grad_up = results[:4]
    return values, grad_hidden, grad_down.T[None], grad_up[None]


def solution(mesh):
    return jax.shard_map(
        per_device,
        mesh=mesh,
        in_specs=(
            P(("groups", "fsdp"), None),
            P(("groups", "fsdp"), None),
            P("fsdp", None),
            P("fsdp", None, None),
            P("fsdp", None, None),
            P(),
            P(("groups", "fsdp"), None),
        ),
        out_specs=(
            P(("groups", "fsdp"), None),
            P(("groups", "fsdp"), None),
            P(("groups", "fsdp"), None, None),
            P(("groups", "fsdp"), None, None),
        ),
        check_vma=False,
    )
```

```python
import functools

import jax
import jax.numpy as jnp
from jax import lax
from jax.experimental import pallas as pl
from jax.experimental.pallas import tpu as pltpu
from jax.sharding import PartitionSpec as P

MESH = pl.DeviceIdType.MESH
adapter_scale = 2.0
F32 = jnp.float32
BF16 = jnp.bfloat16


def dot(a, b, over):
    return lax.dot_general(a, b, ((over[:1], over[1:]), ((), ())), preferred_element_type=F32)


class Ring:
    def __init__(self, place, pool, buf, axis, shared):
        self.place, self.pool, self.buf, self.axis = place, pool, buf, axis
        length = buf.shape[axis]
        self.shared = shared
        self.length = length // 2 if shared else length
        self.start_at = place["side"] * self.length if shared else 0
        self.other_at = (1 - place["side"]) * self.length if shared else 0
        self.right, self.left, self.twin, self.near = {}, {}, {}, {}
        self.near_twin = {}

    def view(self, index, start, length):
        if self.axis == 1:
            return self.buf.at[index, pl.ds(pl.multiple_of(start, 16), length), :]
        return self.buf.at[index, :, pl.ds(pl.multiple_of(start, 128), length)]

    def send(self, index, start, length, to, only=None):
        ref = self.view(index, start, length)
        return self.pool(ref, to, only)

    def chip(self, offset):
        place = self.place
        return place["chip_at"](lax.rem(place["spot"] + offset + place["chips"], place["chips"]))

    def mine(self, offset):
        return self.chip(offset) * 2 + self.place["core"]

    def begin(self):
        place = self.place
        self.near[0] = [self.send(place["me"], 0, self.buf.shape[self.axis], place["near"])]
        self.right[1] = self.send(place["me"], self.start_at, self.length, place["right"])
        self.left[1] = self.send(place["me"], self.start_at, self.length, place["left"])

    def step(self, k, hold_twin=False):
        place, half = self.place, self.length // 2
        last, short = place["chips"] // 2, place["short"]
        from_left, from_right = self.mine(-k), self.mine(k)

        def onward(spot, index, offset, to):
            if k + 1 < last:
                return self.send(index, self.start_at, self.length, to)
            only = jnp.logical_not(place["inner"](spot)) if short else None
            return self.send(index, self.start_at + offset, half, to, only)

        def arrive(copy):
            if k == last and short:
                pl.when(jnp.logical_not(place["inner"](0)))(copy.wait_recv)
            else:
                copy.wait_recv()

        arrive(self.right[k])
        if k < last:
            self.right[k + 1] = onward(1, from_left, 0, place["right"])
        arrive(self.left[k])
        if k < last:
            self.left[k + 1] = onward(-1, from_right, self.length - half, place["left"])
        if short and k == 1:
            self.across = self.send(
                place["facing"], self.start_at, self.length, place["across"], place["inner"](0)
            )
        if short and k == last:
            pl.when(place["inner"](0))(self.across.wait_recv)
        got = self.got(k)
        if self.shared and not hold_twin:
            self.to_twin(k)
        self.near[k] = [self.send(i, self.start_at, self.length, place["near"]) for i in got]

    def got(self, k):
        return [self.mine(-k), self.mine(k)] if k < self.place["chips"] // 2 else [self.mine(-k)]

    def to_twin(self, k):
        to = self.place["twin"]
        self.twin[k] = [self.send(i, self.start_at, self.length, to) for i in self.got(k)]

    def cross(self, k):
        place, got = self.place, self.got(k)
        self.near_twin[k] = []
        for i, copy in zip(got, self.twin[k]):
            copy.wait_recv()
            self.near_twin[k].append(self.send(i, self.other_at, self.length, place["near"]))

    def settle(self, k):
        for copy in self.near[k]:
            copy.wait_recv()
        for copy in self.near_twin.get(k, []):
            copy.wait_recv()


class Direct:
    def __init__(self, place, pool, buf):
        self.place, self.pool, self.buf = place, pool, buf

    def begin(self):
        place = self.place
        ref = self.buf.at[place["me"]]
        self.far = [self.pool(ref, to) for to in place["peers"]]
        self.near = [self.pool(ref, place["near"])]

    def pass_on(self):
        chips = self.place["chips"]
        for offset, copy in enumerate(self.far, 1):
            copy.wait_recv()
            spot = lax.rem(self.place["spot"] - offset + chips, chips)
            ref = self.buf.at[self.place["chip_at"](spot) * 2 + self.place["core"]]
            self.near.append(self.pool(ref, self.place["near"]))

    def settle(self):
        for copy in self.near:
            copy.wait_recv()


def copies_of(chips, shared):
    last = chips // 2
    got = 2 * last - 1
    return 2 + 2 * last + got * (3 if shared else 1)


def kernel(
    n, ring_of, staged,
    owner, tenant, hidden, gradient, weight, down, up,
    values, grad_hidden, grad_down, grad_up, *rest,
):
    if staged:
        parts, w_all, d_all, u_all, t_all, back, stage, send_sems, recv_sems, local_sems = rest
    else:
        parts, w_all, d_all, u_all, t_all, back, send_sems, recv_sems, local_sems = rest
    me = lax.axis_index("fsdp")
    group = lax.axis_index("groups")
    chips, last = n // 2, n // 4
    core, chip = lax.rem(me, 2), me // 2
    chip_at, spot_of = ring_of
    spot = spot_of(chip)
    side = lax.rem(group, 2)

    def device(at):
        return (group, chip_at(lax.rem(spot + at + chips, chips)) * 2 + core)

    peers = [device(at) for at in range(1, chips)]
    short = chips == 8

    def inner(at):
        z = chip_at(lax.rem(spot + at + chips, chips)) // 2
        return (z == 1) | (z == 2)

    facing = (3 - chip // 2) * 4 + lax.rem(chip, 2) * 2 + core
    place = {
        "short": short, "inner": inner, "facing": facing,
        "across": (group, me + 2 - 4 * lax.rem(chip, 2)),
        "peers": peers, "me": me, "core": core, "spot": spot, "side": side, "chips": chips, "chip_at": chip_at,
        "right": device(1), "left": device(-1),
        "near": (group, chip * 2 + 1 - core), "twin": (group + 1 - 2 * side, me),
    }
    local = [
        pltpu.make_async_copy(src, dst.at[me], local_sems.at[i])
        for i, (src, dst) in enumerate(((down, d_all), (weight, w_all)))
    ]
    for copy in local:
        copy.start()

    slot = jnp.int32(0)
    for t in range(owner.shape[0]):
        slot = slot + jnp.where(tenant[0, 0] == t, owner[t], 0)
    rank, width = down.shape
    outputs = gradient.shape[1]
    u_all[me, :, :outputs] = up[...]
    u_all[me, :, outputs:] = jnp.broadcast_to(slot.astype(F32), (rank, 128)).astype(BF16)

    barrier = pltpu.get_barrier_semaphore()
    greeted = [*peers, place["near"], place["twin"]]
    for to in greeted:
        pl.semaphore_signal(barrier, inc=1, device_id=to, device_id_type=MESH)
    pl.semaphore_wait(barrier, len(greeted))

    sent = []

    maybe = []

    def pool(ref, to, only=None):
        i = len(sent) + len(maybe)
        copy = pltpu.make_async_remote_copy(
            src_ref=ref, dst_ref=ref, send_sem=send_sems.at[i], recv_sem=recv_sems.at[i],
            device_id=to, device_id_type=MESH,
        )
        if only is None:
            copy.start()
            sent.append(copy)
        else:
            maybe.append((only, copy))
            pl.when(only)(copy.start)
        return copy

    ups = Direct(place, pool, u_all)
    downs = Ring(place, pool, d_all, 2, True)
    weights = Ring(place, pool, w_all, 1, True)
    terms = Ring(place, pool, parts, 2, False)
    up_terms = Direct(place, pool, t_all)

    local[0].wait()
    downs.begin()
    ups.begin()
    local[1].wait()
    weights.begin()
    downs.step(1)
    ups.pass_on()
    ups.settle()

    tile = 1024
    up_slot = u_all[slot][:, :outputs]
    back_low = (adapter_scale * dot(gradient[...], up_slot, (1, 1))).astype(BF16)
    back[...] = back_low
    back_turned = back_low.astype(F32).T.astype(BF16)
    mine = stage if staged else parts.at[me]

    @pl.loop(0, width // tile)
    def _(t):
        at = pl.ds(pl.multiple_of(t * tile, tile), tile)
        term = dot(back_turned, hidden[:, at], (1, 0))
        mine[:, at] = term.astype(BF16)
        grad_down[:, at] = jnp.zeros((rank, tile), F32)

    if staged:
        out = pltpu.make_async_copy(stage, parts.at[me], local_sems.at[3])
        out.start()
        out.wait()
    terms.begin()

    def chunk(offset, which):
        return chip_at(lax.rem(spot + offset + chips, chips)) * 2 + which

    def share(j):
        return (u_all[j][0:1, outputs:outputs + 1].astype(F32) == me.astype(F32)).astype(F32)

    def add_terms(i, first):
        j = chunk(i // 2 + first, lax.rem(i, 2))
        weight_of = share(j)
        if staged:
            get = pltpu.make_async_copy(parts.at[j], stage, local_sems.at[3])
            get.start()
            get.wait()

        @pl.loop(0, width // tile)
        def _(t):
            at = pl.ds(pl.multiple_of(t * tile, tile), tile)
            term = stage[:, at] if staged else parts[j, :, at]
            grad_down[:, at] += weight_of * term.astype(F32)

    rows = w_all.shape[1]

    def apply_weight(i, total, first):
        j = chunk(i // 2 + first, lax.rem(i, 2))
        at = pl.ds(pl.multiple_of(j * rows, 128), rows)
        block = w_all[j]
        base = dot(gradient[...], block, (1, 1))
        grad_hidden[:, at] = (base + grad_hidden[:, at].astype(F32)).astype(BF16)
        return total + dot(hidden[:, at], block, (1, 0))

    downs.step(2)
    weights.step(1)
    downs.cross(1)
    for k in range(3, last + 1):
        downs.step(k)
        if k > 3:
            weights.to_twin(k - 2)
        terms.step(k - 2)
        weights.step(k - 1, hold_twin=True)
        downs.cross(k - 1)
        if k > 3:
            weights.cross(k - 3)
    weights.to_twin(last - 1)
    downs.cross(last)
    for k in range(last + 1):
        downs.settle(k)

    def low_part(t, total):
        at = pl.ds(pl.multiple_of(t * tile, tile), tile)
        piece = d_all[slot, :, at]
        grad_hidden[:, at] = dot(back[...], piece, (1, 0)).astype(BF16)
        return total + dot(hidden[:, at], piece, (1, 1))

    low = lax.fori_loop(0, width // tile, low_part, jnp.zeros((hidden.shape[0], rank), F32))
    low_turned = low.astype(BF16).astype(F32).T.astype(BF16)
    t_all[me] = (adapter_scale * dot(low_turned, gradient[...], (1, 0))).astype(BF16)
    up_terms.begin()
    total = adapter_scale * dot(low.astype(BF16), u_all[slot][:, :outputs], (1, 0))

    def use(total, first, offsets):
        total = lax.fori_loop(
            0, 2 * offsets, functools.partial(apply_weight, first=first), total
        )

        @pl.loop(0, 2 * offsets)
        def _(i):
            add_terms(i, first)

        return total

    for k in range(last - 2):
        weights.settle(k)
        terms.settle(k)
    total = use(total, 3 - last, 2 * last - 5)
    terms.step(last - 1)
    weights.cross(last - 2)
    weights.step(last)
    weights.settle(last - 2)
    terms.settle(last - 2)
    total = use(total, last - 2, 1)
    total = use(total, 2 - last, 1)
    terms.step(last)
    up_terms.pass_on()
    weights.cross(last - 1)
    weights.settle(last - 1)
    total = lax.fori_loop(0, 2, functools.partial(apply_weight, first=last - 1), total)
    total = lax.fori_loop(0, 2, functools.partial(apply_weight, first=1 - last), total)
    for k in (last - 1, last):
        terms.settle(k)

    @pl.loop(0, 6)
    def _(i):
        add_terms(i, last - 1)

    weights.cross(last)
    weights.settle(last)
    total = lax.fori_loop(0, 2, functools.partial(apply_weight, first=last), total)
    values[...] = total.astype(BF16)
    up_terms.settle()
    grad_up[...] = lax.fori_loop(
        0, n, lambda j, held: held + share(j) * t_all[j].astype(F32),
        jnp.zeros(grad_up.shape, F32),
    )
    for copy in sent:
        copy.wait_send()
    for only, copy in maybe:
        pl.when(only)(copy.wait_send)


def copy_kernel(*refs):
    half = len(refs) // 2
    for source, target in zip(refs[:half], refs[half:]):
        target[...] = source[...]


def ring_order(chips):
    if chips == 8:
        return (
            lambda p: jnp.where(p < 4, 2 * p, 2 * (7 - p) + 1),
            lambda c: jnp.where(lax.rem(c, 2) == 0, c // 2, 7 - c // 2),
        )
    return (lambda p: p, lambda c: c)


def per_device(
    hidden,
    output_gradient,
    frozen_value_weight,
    adapter_down_maps,
    adapter_up_maps,
    owner,
    token_block_tenant,
):
    n = lax.axis_size("fsdp")
    chips = n // 2
    rows, width = hidden.shape
    outputs = output_gradient.shape[1]
    rank = adapter_down_maps.shape[2]
    staged = n > 16
    down = adapter_down_maps[0].T
    count = 2 * copies_of(chips, True) + copies_of(chips, False) + 2 * (2 * chips - 1)
    vmem = pl.BlockSpec(memory_space=pltpu.VMEM)
    smem = pl.BlockSpec(memory_space=pltpu.SMEM)
    hbm = pl.BlockSpec(memory_space=pl.ANY)
    out_shape = [
        jax.ShapeDtypeStruct((rows, outputs), BF16),
        jax.ShapeDtypeStruct((rows, width), BF16),
        jax.ShapeDtypeStruct((rank, width), F32),
        jax.ShapeDtypeStruct((rank, outputs), F32),
    ]
    out_specs = [vmem] * 4
    scratch = []
    if staged:
        out_shape.append(jax.ShapeDtypeStruct((n, rank, width), BF16))
        out_specs.append(hbm)
    else:
        scratch.append(pltpu.VMEM((n, rank, width), BF16))
    scratch += [
        pltpu.VMEM((n,) + frozen_value_weight.shape, BF16),
        pltpu.VMEM((n, rank, width), BF16),
        pltpu.VMEM((n, rank, outputs + 128), BF16),
        pltpu.VMEM((n, rank, outputs), BF16),
        pltpu.VMEM((rows, rank), BF16),
    ]
    if staged:
        scratch.append(pltpu.VMEM((rank, width), BF16))
    scratch += [
        pltpu.SemaphoreType.DMA((count,)),
        pltpu.SemaphoreType.DMA((count,)),
        pltpu.SemaphoreType.DMA((4,)),
    ]
    results = pl.pallas_call(
        functools.partial(kernel, n, ring_order(chips), staged),
        out_shape=out_shape,
        in_specs=[smem, smem, vmem, vmem, hbm, hbm, vmem],
        out_specs=out_specs,
        scratch_shapes=scratch,
        compiler_params=pltpu.CompilerParams(
            collective_id=0, has_side_effects=True, vmem_limit_bytes=56 << 20
        ),
    )(
        owner, token_block_tenant, hidden, output_gradient, frozen_value_weight, down,
        adapter_up_maps[0],
    )
    blocks = [
        pl.BlockSpec((held.shape[0], held.shape[1] // 4), lambda i: (0, i))
        for held in out_shape[:4]
    ]
    values, grad_hidden, grad_down, grad_up = pl.pallas_call(
        copy_kernel, grid=(4,), out_shape=out_shape[:4], in_specs=blocks, out_specs=blocks
    )(*results[:4])
    return values, grad_hidden, grad_down.T[None], grad_up[None]


def solution(mesh):
    return jax.shard_map(
        per_device,
        mesh=mesh,
        in_specs=(
            P(("groups", "fsdp"), None),
            P(("groups", "fsdp"), None),
            P("fsdp", None),
            P("fsdp", None, None),
            P("fsdp", None, None),
            P(),
            P(("groups", "fsdp"), None),
        ),
        out_specs=(
            P(("groups", "fsdp"), None),
            P(("groups", "fsdp"), None),
            P(("groups", "fsdp"), None, None),
            P(("groups", "fsdp"), None, None),
        ),
        check_vma=False,
    )
```

```python
import functools

import jax
import jax.numpy as jnp
from jax import lax
from jax.experimental import pallas as pl
from jax.experimental.pallas import tpu as pltpu
from jax.sharding import PartitionSpec as P

MESH = pl.DeviceIdType.MESH
adapter_scale = 2.0
F32 = jnp.float32
BF16 = jnp.bfloat16


def dot(a, b, over):
    return lax.dot_general(a, b, ((over[:1], over[1:]), ((), ())), preferred_element_type=F32)


class Ring:
    def __init__(self, place, pool, buf, axis, shared):
        self.place, self.pool, self.buf, self.axis = place, pool, buf, axis
        length = buf.shape[axis]
        self.shared = shared
        self.length = length // 2 if shared else length
        self.start_at = place["side"] * self.length if shared else 0
        self.other_at = (1 - place["side"]) * self.length if shared else 0
        self.right, self.left, self.twin, self.near = {}, {}, {}, {}
        self.near_twin = {}

    def view(self, index, start, length):
        if self.axis == 1:
            return self.buf.at[index, pl.ds(pl.multiple_of(start, 16), length), :]
        return self.buf.at[index, :, pl.ds(pl.multiple_of(start, 128), length)]

    def send(self, index, start, length, to, only=None):
        ref = self.view(index, start, length)
        return self.pool(ref, to, only)

    def chip(self, offset):
        place = self.place
        return place["chip_at"](lax.rem(place["spot"] + offset + place["chips"], place["chips"]))

    def mine(self, offset):
        return self.chip(offset) * 2 + self.place["core"]

    def begin(self):
        place = self.place
        self.near[0] = [self.send(place["me"], 0, self.buf.shape[self.axis], place["near"])]
        self.right[1] = self.send(place["me"], self.start_at, self.length, place["right"])
        self.left[1] = self.send(place["me"], self.start_at, self.length, place["left"])

    def step(self, k, hold_twin=False):
        place, half = self.place, self.length // 2
        last, short = place["chips"] // 2, place["short"]
        from_left, from_right = self.mine(-k), self.mine(k)

        def onward(spot, index, offset, to):
            if k + 1 < last:
                return self.send(index, self.start_at, self.length, to)
            only = jnp.logical_not(place["inner"](spot)) if short else None
            return self.send(index, self.start_at + offset, half, to, only)

        def arrive(copy):
            if k == last and short:
                pl.when(jnp.logical_not(place["inner"](0)))(copy.wait_recv)
            else:
                copy.wait_recv()

        arrive(self.right[k])
        if k < last:
            self.right[k + 1] = onward(1, from_left, 0, place["right"])
        arrive(self.left[k])
        if k < last:
            self.left[k + 1] = onward(-1, from_right, self.length - half, place["left"])
        if short and k == 1:
            self.across = self.send(
                place["facing"], self.start_at, self.length, place["across"], place["inner"](0)
            )
        if short and k == last:
            pl.when(place["inner"](0))(self.across.wait_recv)
        got = self.got(k)
        if self.shared and not hold_twin:
            self.to_twin(k)
        self.near[k] = [self.send(i, self.start_at, self.length, place["near"]) for i in got]

    def got(self, k):
        return [self.mine(-k), self.mine(k)] if k < self.place["chips"] // 2 else [self.mine(-k)]

    def to_twin(self, k):
        to = self.place["twin"]
        self.twin[k] = [self.send(i, self.start_at, self.length, to) for i in self.got(k)]

    def cross(self, k):
        place, got = self.place, self.got(k)
        self.near_twin[k] = []
        for i, copy in zip(got, self.twin[k]):
            copy.wait_recv()
            self.near_twin[k].append(self.send(i, self.other_at, self.length, place["near"]))

    def settle(self, k):
        for copy in self.near[k]:
            copy.wait_recv()
        for copy in self.near_twin.get(k, []):
            copy.wait_recv()


class Direct:
    def __init__(self, place, pool, buf):
        self.place, self.pool, self.buf = place, pool, buf

    def begin(self):
        place = self.place
        ref = self.buf.at[place["me"]]
        self.far = [self.pool(ref, to) for to in place["peers"]]
        self.near = [self.pool(ref, place["near"])]

    def pass_on(self):
        chips = self.place["chips"]
        for offset, copy in enumerate(self.far, 1):
            copy.wait_recv()
            spot = lax.rem(self.place["spot"] - offset + chips, chips)
            ref = self.buf.at[self.place["chip_at"](spot) * 2 + self.place["core"]]
            self.near.append(self.pool(ref, self.place["near"]))

    def settle(self):
        for copy in self.near:
            copy.wait_recv()


def copies_of(chips, shared):
    last = chips // 2
    got = 2 * last - 1
    return 2 + 2 * last + got * (3 if shared else 1)


def kernel(
    n, ring_of, staged,
    owner, tenant, hidden, gradient, weight, down, up,
    values, grad_hidden, grad_down, grad_up, *rest,
):
    if staged:
        parts, w_all, d_all, u_all, t_all, back, stage, send_sems, recv_sems, local_sems = rest
    else:
        parts, w_all, d_all, u_all, t_all, back, send_sems, recv_sems, local_sems = rest
    me = lax.axis_index("fsdp")
    group = lax.axis_index("groups")
    chips, last = n // 2, n // 4
    core, chip = lax.rem(me, 2), me // 2
    chip_at, spot_of = ring_of
    spot = spot_of(chip)
    side = lax.rem(group, 2)

    def device(at):
        return (group, chip_at(lax.rem(spot + at + chips, chips)) * 2 + core)

    peers = [device(at) for at in range(1, chips)]
    short = chips == 8

    def inner(at):
        z = chip_at(lax.rem(spot + at + chips, chips)) // 2
        return (z == 1) | (z == 2)

    facing = (3 - chip // 2) * 4 + lax.rem(chip, 2) * 2 + core
    place = {
        "short": short, "inner": inner, "facing": facing,
        "across": (group, me + 2 - 4 * lax.rem(chip, 2)),
        "peers": peers, "me": me, "core": core, "spot": spot, "side": side, "chips": chips, "chip_at": chip_at,
        "right": device(1), "left": device(-1),
        "near": (group, chip * 2 + 1 - core), "twin": (group + 1 - 2 * side, me),
    }
    local = [
        pltpu.make_async_copy(src, dst.at[me], local_sems.at[i])
        for i, (src, dst) in enumerate(((down, d_all), (weight, w_all)))
    ]
    for copy in local:
        copy.start()

    slot = jnp.int32(0)
    for t in range(owner.shape[0]):
        slot = slot + jnp.where(tenant[0, 0] == t, owner[t], 0)
    rank, width = down.shape
    outputs = gradient.shape[1]
    u_all[me, :, :outputs] = up[...]
    u_all[me, :, outputs:] = jnp.broadcast_to(slot.astype(F32), (rank, 128)).astype(BF16)

    barrier = pltpu.get_barrier_semaphore()
    greeted = [*peers, place["near"], place["twin"]]
    for to in greeted:
        pl.semaphore_signal(barrier, inc=1, device_id=to, device_id_type=MESH)
    pl.semaphore_wait(barrier, len(greeted))

    sent = []

    maybe = []

    def pool(ref, to, only=None):
        i = len(sent) + len(maybe)
        copy = pltpu.make_async_remote_copy(
            src_ref=ref, dst_ref=ref, send_sem=send_sems.at[i], recv_sem=recv_sems.at[i],
            device_id=to, device_id_type=MESH,
        )
        if only is None:
            copy.start()
            sent.append(copy)
        else:
            maybe.append((only, copy))
            pl.when(only)(copy.start)
        return copy

    ups = Direct(place, pool, u_all)
    downs = Ring(place, pool, d_all, 2, True)
    weights = Ring(place, pool, w_all, 1, True)
    terms = Ring(place, pool, parts, 2, False)
    up_terms = Direct(place, pool, t_all)

    local[0].wait()
    downs.begin()
    ups.begin()
    local[1].wait()
    weights.begin()
    downs.step(1)
    ups.pass_on()
    ups.settle()

    tile = 1024
    up_slot = u_all[slot][:, :outputs]
    back_low = (adapter_scale * dot(gradient[...], up_slot, (1, 1))).astype(BF16)
    back[...] = back_low
    back_turned = back_low.astype(F32).T.astype(BF16)
    mine = stage if staged else parts.at[me]

    @pl.loop(0, width // tile)
    def _(t):
        at = pl.ds(pl.multiple_of(t * tile, tile), tile)
        term = dot(back_turned, hidden[:, at], (1, 0))
        mine[:, at] = term.astype(BF16)
        grad_down[:, at] = jnp.zeros((rank, tile), F32)

    if staged:
        out = pltpu.make_async_copy(stage, parts.at[me], local_sems.at[3])
        out.start()
        out.wait()
    terms.begin()

    def chunk(offset, which):
        return chip_at(lax.rem(spot + offset + chips, chips)) * 2 + which

    def share(j):
        return (u_all[j][0:1, outputs:outputs + 1].astype(F32) == me.astype(F32)).astype(F32)

    def add_terms(i, first):
        pair = [chunk(i + first, 0), chunk(i + first, 1)]
        for group in [[j] for j in pair] if staged else [pair]:
            weights_of = [share(j) for j in group]
            if staged:
                get = pltpu.make_async_copy(parts.at[group[0]], stage, local_sems.at[3])
                get.start()
                get.wait()

            @pl.loop(0, width // tile)
            def _(t):
                at = pl.ds(pl.multiple_of(t * tile, tile), tile)
                total = grad_down[:, at]
                for weight_of, j in zip(weights_of, group):
                    term = stage[:, at] if staged else parts[j, :, at]
                    total = total + weight_of * term.astype(F32)
                grad_down[:, at] = total

    rows = w_all.shape[1]

    def apply_weight(i, total, first):
        j = chunk(i + first, 0)
        at = pl.ds(pl.multiple_of(j * rows, 128), 2 * rows)
        block = w_all[pl.ds(j, 2)].reshape(2 * rows, outputs)
        base = dot(gradient[...], block, (1, 1))
        grad_hidden[:, at] = (base + grad_hidden[:, at].astype(F32)).astype(BF16)
        return total + dot(hidden[:, at], block, (1, 0))

    downs.step(2)
    weights.step(1)
    downs.cross(1)
    for k in range(3, last + 1):
        downs.step(k)
        if k > 3:
            weights.to_twin(k - 2)
        terms.step(k - 2)
        weights.step(k - 1, hold_twin=True)
        downs.cross(k - 1)
        if k > 3:
            weights.cross(k - 3)
    weights.to_twin(last - 1)
    downs.cross(last)
    for k in range(last + 1):
        downs.settle(k)

    def low_part(t, total):
        at = pl.ds(pl.multiple_of(t * tile, tile), tile)
        piece = d_all[slot, :, at]
        grad_hidden[:, at] = dot(back[...], piece, (1, 0)).astype(BF16)
        return total + dot(hidden[:, at], piece, (1, 1))

    low = lax.fori_loop(0, width // tile, low_part, jnp.zeros((hidden.shape[0], rank), F32))
    low_turned = low.astype(BF16).astype(F32).T.astype(BF16)
    t_all[me] = (adapter_scale * dot(low_turned, gradient[...], (1, 0))).astype(BF16)
    up_terms.begin()
    total = adapter_scale * dot(low.astype(BF16), u_all[slot][:, :outputs], (1, 0))

    def use(total, first, offsets):
        total = lax.fori_loop(
            0, offsets, functools.partial(apply_weight, first=first), total
        )

        @pl.loop(0, offsets)
        def _(i):
            add_terms(i, first)

        return total

    for k in range(last - 2):
        weights.settle(k)
        terms.settle(k)
    total = use(total, 3 - last, 2 * last - 5)
    terms.step(last - 1)
    weights.cross(last - 2)
    weights.step(last)
    weights.settle(last - 2)
    terms.settle(last - 2)
    total = use(total, last - 2, 1)
    total = use(total, 2 - last, 1)
    terms.step(last)
    up_terms.pass_on()
    weights.cross(last - 1)
    weights.settle(last - 1)
    total = lax.fori_loop(0, 1, functools.partial(apply_weight, first=last - 1), total)
    total = lax.fori_loop(0, 1, functools.partial(apply_weight, first=1 - last), total)
    for k in (last - 1, last):
        terms.settle(k)

    @pl.loop(0, 3)
    def _(i):
        add_terms(i, last - 1)

    weights.cross(last)
    weights.settle(last)
    total = lax.fori_loop(0, 1, functools.partial(apply_weight, first=last), total)
    values[...] = total.astype(BF16)
    up_terms.settle()
    grad_up[...] = lax.fori_loop(
        0, n, lambda j, held: held + share(j) * t_all[j].astype(F32),
        jnp.zeros(grad_up.shape, F32),
    )
    for copy in sent:
        copy.wait_send()
    for only, copy in maybe:
        pl.when(only)(copy.wait_send)


def copy_kernel(*refs):
    half = len(refs) // 2
    for source, target in zip(refs[:half], refs[half:]):
        target[...] = source[...]


def ring_order(chips):
    if chips == 8:
        return (
            lambda p: jnp.where(p < 4, 2 * p, 2 * (7 - p) + 1),
            lambda c: jnp.where(lax.rem(c, 2) == 0, c // 2, 7 - c // 2),
        )
    return (lambda p: p, lambda c: c)


def per_device(
    hidden,
    output_gradient,
    frozen_value_weight,
    adapter_down_maps,
    adapter_up_maps,
    owner,
    token_block_tenant,
):
    n = lax.axis_size("fsdp")
    chips = n // 2
    rows, width = hidden.shape
    outputs = output_gradient.shape[1]
    rank = adapter_down_maps.shape[2]
    staged = n > 16
    down = adapter_down_maps[0].T
    count = 2 * copies_of(chips, True) + copies_of(chips, False) + 2 * (2 * chips - 1)
    vmem = pl.BlockSpec(memory_space=pltpu.VMEM)
    smem = pl.BlockSpec(memory_space=pltpu.SMEM)
    hbm = pl.BlockSpec(memory_space=pl.ANY)
    out_shape = [
        jax.ShapeDtypeStruct((rows, outputs), BF16),
        jax.ShapeDtypeStruct((rows, width), BF16),
        jax.ShapeDtypeStruct((rank, width), F32),
        jax.ShapeDtypeStruct((rank, outputs), F32),
    ]
    out_specs = [vmem] * 4
    scratch = []
    if staged:
        out_shape.append(jax.ShapeDtypeStruct((n, rank, width), BF16))
        out_specs.append(hbm)
    else:
        scratch.append(pltpu.VMEM((n, rank, width), BF16))
    scratch += [
        pltpu.VMEM((n,) + frozen_value_weight.shape, BF16),
        pltpu.VMEM((n, rank, width), BF16),
        pltpu.VMEM((n, rank, outputs + 128), BF16),
        pltpu.VMEM((n, rank, outputs), BF16),
        pltpu.VMEM((rows, rank), BF16),
    ]
    if staged:
        scratch.append(pltpu.VMEM((rank, width), BF16))
    scratch += [
        pltpu.SemaphoreType.DMA((count,)),
        pltpu.SemaphoreType.DMA((count,)),
        pltpu.SemaphoreType.DMA((4,)),
    ]
    results = pl.pallas_call(
        functools.partial(kernel, n, ring_order(chips), staged),
        out_shape=out_shape,
        in_specs=[smem, smem, vmem, vmem, hbm, hbm, vmem],
        out_specs=out_specs,
        scratch_shapes=scratch,
        compiler_params=pltpu.CompilerParams(
            collective_id=0, has_side_effects=True, vmem_limit_bytes=56 << 20
        ),
    )(
        owner, token_block_tenant, hidden, output_gradient, frozen_value_weight, down,
        adapter_up_maps[0],
    )
    blocks = [
        pl.BlockSpec((held.shape[0], held.shape[1] // 4), lambda i: (0, i))
        for held in out_shape[:4]
    ]
    values, grad_hidden, grad_down, grad_up = pl.pallas_call(
        copy_kernel, grid=(4,), out_shape=out_shape[:4], in_specs=blocks, out_specs=blocks
    )(*results[:4])
    return values, grad_hidden, grad_down.T[None], grad_up[None]


def solution(mesh):
    return jax.shard_map(
        per_device,
        mesh=mesh,
        in_specs=(
            P(("groups", "fsdp"), None),
            P(("groups", "fsdp"), None),
            P("fsdp", None),
            P("fsdp", None, None),
            P("fsdp", None, None),
            P(),
            P(("groups", "fsdp"), None),
        ),
        out_specs=(
            P(("groups", "fsdp"), None),
            P(("groups", "fsdp"), None),
            P(("groups", "fsdp"), None, None),
            P(("groups", "fsdp"), None, None),
        ),
        check_vma=False,
    )
```
